256 devices in a mesh: span: 16 (over z_hi, x), tok: 16 (over y, z_lo, core).
Axes of the slice: x: 4, y: 4, z: 8 (z_hi: 4, z_lo: 2; z = z_hi * 2 + z_lo), core: 2. Of those that a mesh axis runs over, the one named last changes fastest.
Arguments:
- latents: float32 [96, 1024, 640], P('span', 'tok'), may hold values from -6 to 6
- lengths: int32 [16], replicated, may hold values from 1 to 6, 64 in all
- intersection: int32 [16], replicated, may hold values from 1 to 4, as said below
- spatial_query: bfloat16 [640, 640], replicated, may hold values from -3 to 3
- spatial_key: bfloat16 [640, 640], replicated, may hold values from -0.25 to 0.25
- spatial_value: bfloat16 [640, 640], replicated, may hold values from -0.25 to 0.25
- spatial_out: bfloat16 [640, 640], replicated, may hold values from -0.25 to 0.25
- temporal_query: bfloat16 [640, 640], replicated, may hold values from -3 to 3
- temporal_key: bfloat16 [640, 640], replicated, may hold values from -0.25 to 0.25
- temporal_value: bfloat16 [640, 640], replicated, may hold values from -0.25 to 0.25
- temporal_out: bfloat16 [640, 640], replicated, may hold values from -0.25 to 0.25
- feed_value: bfloat16 [640, 2560], P(None, 'span'), may hold values from -0.25 to 0.25
- feed_gate: bfloat16 [640, 2560], P(None, 'span'), may hold values from -0.25 to 0.25
- feed_down: bfloat16 [640, 2560], P(None, 'span'), may hold values from -0.125 to 0.125
Outputs:
- refined: float32 [96, 1024, 640], P('span', 'tok')
The draws below stay inside these ranges and needn't reach their ends.
Inputs may be any that keep to these rules, and one draw needn't show every extreme that they name: `lengths`: the frames of all spans sum to 4 * 16; some span has exactly 6. `intersection`: some span takes exactly 4 in every draw.
All inputs are finite; a program needn't handle non-finite values.
Results may differ from the reference program's by a relative error of at most 0.014.
The reference program's roundings to bfloat16 on the way count: a program that leaves them out, or rounds other values in their place, can miss the bound.
Values may be sent and summed in bfloat16 or wider, within the bound.
No kernel may reach another device: no remote copies, remote signals or barrier semaphores. Data moves between devices by JAX's collectives and lax.ppermute only.
A program may use at most 192 MiB of HBM per device.

```python
import math
import jax
import jax.numpy as jnp
import numpy as np
from jax import lax

C = 640
HEADS = 8
HID = 2560
CAP = 6
FR_MEAN = 4
OVL = 4
PIXELS = 1024
SLOTS = 96
N_SPAN = 16


def query_matrix(base_key, lowest, highest):
    entry_key, head_key = jax.random.split(base_key)
    entries = jax.random.normal(entry_key, (C, C), jnp.float32) * C ** (-0.5)
    factors = jnp.exp(jax.random.uniform(head_key, (HEADS,), jnp.float32, math.log(lowest), math.log(highest)))
    columns = jnp.repeat(factors, C // HEADS)
    return jnp.clip(entries * columns[None, :], -3.0, 3.0).astype(jnp.bfloat16)


def draw_intersection(key, part):
    key = jax.random.fold_in(key, 7)
    width_key, place_key = jax.random.split(key)
    widths = jax.random.randint(width_key, (N_SPAN,), 1, OVL + 1)
    chosen = jax.random.randint(place_key, (), 0, N_SPAN)
    return jnp.where(jnp.arange(N_SPAN) == chosen, OVL, widths).astype(jnp.int32)


def draw_spatial_query(key, part):
    key = jax.random.fold_in(key, 11)
    return query_matrix(key, 0.5, 2.0)


def draw_temporal_query(key, part):
    key = jax.random.fold_in(key, 13)
    return query_matrix(key, 0.5, 2.0)


def block_levels(own_key, shape, cuts, least, top_value):
    factor_of, own = 1.0, jax.random.fold_in(own_key, 6)
    for axis_at, blocks in cuts:
        draws = jnp.exp(jax.random.uniform(jax.random.fold_in(own, axis_at), (blocks,), jnp.float32, least / len(cuts), top_value / len(cuts)))
        factor_of = factor_of * jnp.repeat(draws, shape[axis_at] // blocks).reshape([-1 if axis == axis_at else 1 for axis in range(len(shape))])
    return factor_of


def split_up(amount, total, bound, slope):
    weights = [(1 << 20) // math.isqrt(rank ** slope) + 1 for rank in range(2, amount + 1)]
    spare, counts = total - bound - (amount - 1), [1] * (amount - 1)
    while spare > 0:
        free = [i for i in range(amount - 1) if counts[i] < bound]
        whole, remaining = sum([weights[i] for i in free]), spare
        for i in free:
            addition = min(bound - counts[i], max(1, remaining * weights[i] // whole), spare)
            counts[i] = counts[i] + addition
            spare = spare - addition
    return np.array([bound] + counts)


def uneven_parts(own_key, number_of, total, limit, skew):
    if number_of == 2:
        one = jax.random.randint(own_key, (), max(1, total - limit), min(limit, total - 1) + 1)
        return jnp.stack([one, total - one])
    tallies = jnp.asarray(split_up(number_of, total, limit, skew), jnp.int32)
    twos = (number_of - 1) // 2
    donor, sink = tallies[1:1 + 2 * twos:2], tallies[2:2 + 2 * twos:2]
    slack = jnp.minimum(donor - 1, limit - sink)
    moved = jax.random.randint(jax.random.fold_in(own_key, 1), (twos,), 0, 1 << 20) % (slack + 1)
    tallies = tallies.at[1:1 + 2 * twos:2].set(donor - moved).at[2:2 + 2 * twos:2].set(sink + moved)
    return tallies[jax.random.permutation(jax.random.fold_in(own_key, 2), number_of)]


def noise(stream_key, extent, scale, reach, cuts=(), kind=jnp.bfloat16):
    factor_of = block_levels(stream_key, extent, cuts, -0.22, 0.18) if cuts else 1.0
    array = jax.random.normal(stream_key, extent, jnp.float32) * scale * factor_of
    return jnp.minimum(jnp.maximum(array, -reach), reach).astype(kind)


def setup_inputs(seed: int = 0) -> dict:
    key_of = jax.random.split(jax.random.key(seed), 15)
    latents = noise(key_of[0], (SLOTS, PIXELS, C), 1.0, 6.0, ((0, 16), (1, 16)), jnp.float32)
    lengths = uneven_parts(key_of[1], N_SPAN, FR_MEAN * N_SPAN, CAP, 2).astype(jnp.int32)
    intersection = draw_intersection(jax.random.fold_in(key_of[14], 71), 0)
    spatial_query = draw_spatial_query(jax.random.fold_in(key_of[14], 71), 0)
    spatial_key = noise(key_of[4], (C, C), C ** -0.5, 0.25)
    spatial_value = noise(key_of[5], (C, C), C ** -0.5, 0.25)
    spatial_out = noise(key_of[6], (C, C), C ** -0.5, 0.25)
    temporal_query = draw_temporal_query(jax.random.fold_in(key_of[14], 71), 0)
    temporal_key = noise(key_of[8], (C, C), C ** -0.5, 0.25)
    temporal_value = noise(key_of[9], (C, C), C ** -0.5, 0.25)
    temporal_out = noise(key_of[10], (C, C), C ** -0.5, 0.25)
    feed_value = noise(key_of[11], (C, HID), C ** -0.5, 0.25, ((1, 16),))
    feed_gate = noise(key_of[12], (C, HID), C ** -0.5, 0.25, ((1, 16),))
    feed_down = noise(key_of[13], (C, HID), HID ** -0.5, 0.125, ((1, 16),))
    return dict(latents=latents, lengths=lengths, intersection=intersection, spatial_query=spatial_query, spatial_key=spatial_key, spatial_value=spatial_value, spatial_out=spatial_out, temporal_query=temporal_query, temporal_key=temporal_key, temporal_value=temporal_value, temporal_out=temporal_out, feed_value=feed_value, feed_gate=feed_gate, feed_down=feed_down)


def layer_norm(values):
    center = values - lax.optimization_barrier(jnp.mean(values, axis=-1, keepdims=True))
    spread = lax.optimization_barrier(jnp.mean(center * center, axis=-1, keepdims=True))
    return (center * lax.rsqrt(spread + 1e-05)).astype(jnp.bfloat16)

def softmax_rows(scores, allowed):
    masked = jnp.where(allowed, scores, -1e+30)
    highest = lax.optimization_barrier(jnp.max(masked, axis=-1, keepdims=True))
    raised = jnp.where(allowed, jnp.exp(masked - highest), 0.0)
    return (raised / lax.optimization_barrier(jnp.sum(raised, axis=-1, keepdims=True))).astype(jnp.bfloat16)

def reference(latents, lengths, intersection, spatial_query, spatial_key, spatial_value, spatial_out, temporal_query, temporal_key, temporal_value, temporal_out, feed_value, feed_gate, feed_down):
    slot_count, pixels, channels = latents.shape
    head_size = channels // HEADS
    scaling = head_size ** (-0.5)
    groups = lengths.shape[0]

    def project(normed, matrix):
        return jnp.dot(normed, matrix, preferred_element_type=jnp.float32).astype(jnp.bfloat16)

    def spatial(frame):
        normed = layer_norm(frame)
        queries = project(normed, spatial_query).reshape(pixels, HEADS, head_size).astype(jnp.float32)
        keys_here = project(normed, spatial_key).reshape(pixels, HEADS, head_size).astype(jnp.float32)
        values_here = project(normed, spatial_value).reshape(pixels, HEADS, head_size).astype(jnp.float32)
        scores = jnp.einsum('phd,khd->hpk', queries, keys_here) * scaling
        weights = softmax_rows(scores, True)
        context = jnp.einsum('hpk,khd->phd', weights.astype(jnp.float32), values_here)
        context = context.astype(jnp.bfloat16).reshape(pixels, channels)
        return frame + jnp.dot(context, spatial_out, preferred_element_type=jnp.float32)
    middle = lax.map(spatial, latents)
    second = layer_norm(middle).reshape(slot_count * pixels, channels)
    time_queries = project(second, temporal_query).reshape(groups, CAP, pixels, channels)
    time_keys = project(second, temporal_key).reshape(groups, CAP, pixels, channels)
    time_values = project(second, temporal_value).reshape(groups, CAP, pixels, channels)
    offsets = jnp.arange(OVL, dtype=jnp.int32)
    positions = jnp.arange(CAP, dtype=jnp.int32)

    def temporal(group):
        before = jnp.maximum(group - 1, 0)
        after = jnp.minimum(group + 1, groups - 1)
        own_length = lengths[group]
        prev_length = lengths[before]
        next_length = lengths[after]
        borrow = intersection[group]
        prev_slots = prev_length - OVL + offsets
        tail_slots = jnp.maximum(prev_slots, 0)

        def window(source):
            return jnp.concatenate([source[before][tail_slots], source[group], source[after][:OVL]], axis=0)
        key_window = window(time_keys).reshape(CAP + 2 * OVL, pixels, HEADS, head_size).astype(jnp.float32)
        value_window = window(time_values).reshape(CAP + 2 * OVL, pixels, HEADS, head_size).astype(jnp.float32)
        allowed = jnp.concatenate([(group > 0) & (prev_slots >= 0) & (offsets >= OVL - borrow), positions < own_length, (group < groups - 1) & (offsets < next_length) & (offsets < borrow)])
        queries = time_queries[group].reshape(CAP, pixels, HEADS, head_size).astype(jnp.float32)
        scores = jnp.einsum('fphd,sphd->phfs', queries, key_window) * scaling
        weights = softmax_rows(scores, allowed)
        context = jnp.einsum('phfs,sphd->fphd', weights.astype(jnp.float32), value_window)
        return context.astype(jnp.bfloat16).reshape(CAP, pixels, channels)
    contexts = lax.map(temporal, jnp.arange(groups, dtype=jnp.int32))
    late = middle + jnp.dot(contexts.reshape(slot_count * pixels, channels), temporal_out, preferred_element_type=jnp.float32).reshape(slot_count, pixels, channels)

    def feed(frame):
        third = layer_norm(frame)
        hidden = jnp.dot(third, feed_value, preferred_element_type=jnp.float32) * jax.nn.gelu(jnp.dot(third, feed_gate, preferred_element_type=jnp.float32), approximate=False)
        hidden = hidden.astype(jnp.bfloat16)
        return frame + jnp.dot(hidden, feed_down.T, preferred_element_type=jnp.float32)
    refined = lax.map(feed, late)
    live = jnp.arange(slot_count, dtype=jnp.int32) % CAP < jnp.repeat(lengths, CAP)
    return jnp.where(live[:, None, None], refined, 0.0)
```

```python
import functools

import jax
import jax.numpy as jnp
from jax import lax
from jax.experimental import pallas as pl
from jax.experimental.pallas import tpu as pltpu
from jax.sharding import Mesh
from jax.sharding import PartitionSpec as P

HEADS = 8
OVL = 4
HS = 80
C = 640
FR = 6
HALF = 3
PX = 64
TOKS = 16
PAIR = 16
F32 = jnp.float32
BF16 = jnp.bfloat16
SPAN = ("zh", "x")
TOK = ("y", "zl", "c")
SCALE = HS ** (-0.5)
VMEM = pltpu.VMEM
SMEM = pltpu.SMEM
LAYOUT = ((80, 160, 0), (0, 160, 80), (0, 80, 160))


def params(mib=48):
    return pltpu.CompilerParams(vmem_limit_bytes=mib * 1024 * 1024)


def vm(n):
    return [pl.BlockSpec(memory_space=VMEM)] * n


def cost(flops, nbytes, exps=0):
    return pl.CostEstimate(flops=flops, bytes_accessed=nbytes, transcendentals=exps)


def dot(a, b):
    return jnp.dot(a, b, preferred_element_type=F32)


def dot_t(a, b):
    return lax.dot_general(a, b, (((1,), (1,)), ((), ())), preferred_element_type=F32)


def layer_norm(values):
    center = values - jnp.mean(values, axis=-1, keepdims=True)
    spread = jnp.mean(center * center, axis=-1, keepdims=True)
    return (center * lax.rsqrt(spread + 1e-05)).astype(BF16)


def lanes(shape, start, width):
    lane = lax.broadcasted_iota(jnp.int32, shape, len(shape) - 1)
    return (lane >= start) & (lane < start + width)


def qkv_kernel(x_ref, wq_ref, wk_ref, wv_ref, out_ref):
    normed = layer_norm(x_ref[...].reshape(HALF * PX, C))
    q = dot(normed, wq_ref[...]).astype(BF16)
    k = dot(normed, wk_ref[...]).astype(BF16)
    v = dot(normed, wv_ref[...]).astype(BF16)
    pad = jnp.zeros((PX, 256 - 3 * HS), BF16)
    for h in range(HEADS):
        cols = slice(h * HS, (h + 1) * HS)
        for f in range(HALF):
            rows = slice(f * PX, (f + 1) * PX)
            order = sorted(zip(LAYOUT[f], (q, k, v)), key=lambda e: e[0])
            parts = [arr[rows, cols] for _, arr in order] + [pad]
            out_ref[h, rows, :] = jnp.concatenate(parts, axis=1)


def spatial_kernel(x_ref, out_ref, k_ref):
    n = TOKS * PX
    qb = 256
    dst = qb // PX
    for f in range(HALF):
        q_at, k_at, v_at = LAYOUT[f]
        rows = slice(f * PX, (f + 1) * PX)
        x = x_ref[:, rows, :].reshape(n, 256)
        k_ref[...] = pltpu.roll(x.astype(F32), (q_at - k_at) % 256, 1).astype(BF16)

        def block(i, _, rows=rows, q_at=q_at, v_at=v_at, f=f):
            xq = x_ref[pl.ds(i * dst, dst), rows, :].reshape(qb, 256)
            xq = jnp.where(lanes((qb, 256), q_at, HS), xq, jnp.zeros_like(xq))
            s = dot_t(xq, k_ref[...])
            top = jnp.max(s, axis=-1, keepdims=True)
            e = jnp.exp((s - top) * SCALE)
            r = 1.0 / jnp.sum(e, axis=-1, keepdims=True)
            p = (e * r).astype(BF16)
            ctx = dot(p, x_ref[:, rows, :].reshape(n, 256)).astype(BF16)
            if f > 0:
                old = out_ref[pl.ds(i * dst, dst)].reshape(qb, 256)
                ctx = jnp.where(lanes((qb, 256), v_at, HS), ctx, old)
            out_ref[pl.ds(i * dst, dst)] = ctx.reshape(dst, PX, 256)
            return 0

        lax.fori_loop(0, n // qb, block, 0)


def middle_kernel(len_ref, at_ref, ctx_ref, x_ref, w_ref, mid_ref, second_ref, head_ref, tail_ref):
    rows = []
    for half in range(2):
        for f in range(HALF):
            cols = slice(f * HS, (f + 1) * HS)
            rows.append(jnp.concatenate([ctx_ref[half * HEADS + h, :, cols] for h in range(HEADS)], axis=1))
    context = jnp.concatenate(rows, axis=0)
    middle = x_ref[...].reshape(FR * PX, C) + dot(context, w_ref[...])
    mid_ref[...] = middle
    second = layer_norm(middle).reshape(FR, PX, C)
    second_ref[...] = second
    head_ref[...] = second[:OVL]
    own = len_ref[at_ref[0]]
    for j in range(OVL):
        at = jnp.maximum(own - OVL + j, 0)
        tail_ref[j] = second_ref[at]


def time_kernel(s_ref, wq_ref, wk_ref, wv_ref, q_ref, k_ref, v_ref):
    second = s_ref[...].reshape(FR * PX, C)
    q_ref[...] = dot(second, wq_ref[...]).astype(BF16).reshape(FR, PX, C)
    k_ref[...] = dot(second, wk_ref[...]).astype(BF16).reshape(FR, PX, C)
    v_ref[...] = dot(second, wv_ref[...]).astype(BF16).reshape(FR, PX, C)


def temporal_kernel(
    len_ref, inter_ref, at_ref, q_ref, k_ref, v_ref, prev_ref, next_ref, mid_ref, wk_ref, wv_ref, wo_ref,
    late_ref, third_ref, kw_ref, vw_ref, ctx_ref,
):
    me = at_ref[0]
    spans = len_ref.shape[0]
    own = len_ref[me]
    prev_len = len_ref[jnp.maximum(me - 1, 0)]
    next_len = len_ref[jnp.minimum(me + 1, spans - 1)]
    borrow = inter_ref[me]
    prev = prev_ref[...].reshape(OVL * PX, C)
    after = next_ref[...].reshape(OVL * PX, C)
    kw_ref[:OVL] = dot(prev, wk_ref[...]).astype(BF16).reshape(OVL, PX, C)
    kw_ref[OVL : OVL + FR] = k_ref[...]
    kw_ref[OVL + FR :] = dot(after, wk_ref[...]).astype(BF16).reshape(OVL, PX, C)
    vw_ref[:OVL] = dot(prev, wv_ref[...]).astype(BF16).reshape(OVL, PX, C)
    vw_ref[OVL : OVL + FR] = v_ref[...]
    vw_ref[OVL + FR :] = dot(after, wv_ref[...]).astype(BF16).reshape(OVL, PX, C)

    window = FR + 2 * OVL
    nrow, ncol = FR * PAIR, window * PAIR
    col = lax.broadcasted_iota(jnp.int32, (nrow, ncol), 1)
    row = lax.broadcasted_iota(jnp.int32, (nrow, ncol), 0)
    slot = col // PAIR
    low_prev = jnp.where(me > 0, jnp.maximum(OVL - borrow, OVL - prev_len), OVL)
    high_next = jnp.where(me < spans - 1, jnp.minimum(borrow, next_len), 0)
    live = ((slot >= low_prev) & (slot < OVL + own)) | ((slot >= OVL + FR) & (slot < OVL + FR + high_next))
    allowed = live & ((col % PAIR) == (row % PAIR))

    for g in range(PX // PAIR):
        at = slice(g * PAIR, (g + 1) * PAIR)
        qg = q_ref[:, at, :].reshape(nrow, C)
        kg = kw_ref[:, at, :].reshape(ncol, C)
        vg = vw_ref[:, at, :].reshape(ncol, C)
        acc = [jnp.zeros((nrow, 128), F32) for _ in range(C // 128)]
        for h in range(HEADS):
            t0, t1 = h * HS // 128, -(-(h + 1) * HS // 128)
            base, width = t0 * 128, (t1 - t0) * 128
            mask = lanes((nrow, width), h * HS - base, HS)
            qh = qg[:, base : base + width]
            qh = jnp.where(mask, qh, jnp.zeros_like(qh))
            s = dot_t(qh, kg[:, base : base + width])
            s = jnp.where(allowed, s, -1e30)
            top = jnp.max(s, axis=-1, keepdims=True)
            e = jnp.where(allowed, jnp.exp((s - top) * SCALE), 0.0)
            p = (e * (1.0 / jnp.sum(e, axis=-1, keepdims=True))).astype(BF16)
            part = jnp.where(mask, dot(p, vg[:, base : base + width]), 0.0)
            for t in range(t0, t1):
                acc[t] = acc[t] + part[:, (t - t0) * 128 : (t - t0 + 1) * 128]
        context = jnp.concatenate(acc, axis=1).astype(BF16)
        ctx_ref[:, at, :] = context.reshape(FR, PAIR, C)
    late = mid_ref[...] + dot(ctx_ref[...].reshape(FR * PX, C), wo_ref[...])
    late_ref[...] = late
    third_ref[...] = layer_norm(late)


def feed_kernel(last, *refs):
    if last:
        len_ref, at_ref, third_ref, base_ref, w_ref, out_ref = refs
    else:
        third_ref, base_ref, w_ref, out_ref = refs
    step = pl.program_id(0)
    shards = w_ref.shape[0]
    units = w_ref.shape[2]

    def piece(i):
        return w_ref[:, i].reshape(shards * units, C)

    third = third_ref[...]
    gate = dot_t(third, piece(1))
    gate = 0.5 * gate * (1.0 + lax.erf(gate * (0.5**0.5)))
    hidden = (dot_t(third, piece(0)) * gate).astype(BF16)
    part = dot(hidden, piece(2))

    @pl.when(step == 0)
    def _():
        out_ref[...] = base_ref[...] + part

    @pl.when(step > 0)
    def _():
        out_ref[...] += part

    if last:
        @pl.when(step == pl.num_programs(0) - 1)
        def _():
            own = len_ref[at_ref[0]]
            row = lax.broadcasted_iota(jnp.int32, out_ref.shape, 0)
            out_ref[...] = jnp.where(row < own * PX, out_ref[...], 0.0)


def feed(third, base, weights, scalars, steps=2):
    rows = FR * PX
    shards, kinds, units, _ = weights.shape
    last = scalars is not None
    specs = [
        pl.BlockSpec((rows, C), lambda i: (0, 0)),
        pl.BlockSpec((rows, C), lambda i: (0, 0)),
        pl.BlockSpec((shards // steps, kinds, units, C), lambda i: (i, 0, 0, 0)),
    ]
    if last:
        specs = [pl.BlockSpec(memory_space=SMEM)] * 2 + specs
    return pl.pallas_call(
        functools.partial(feed_kernel, last),
        grid=(steps,),
        in_specs=specs,
        out_specs=pl.BlockSpec((rows, C), lambda i: (0, 0)),
        out_shape=jax.ShapeDtypeStruct((rows, C), F32),
        compiler_params=params(),
        cost_estimate=cost(2 * rows * C * shards * units * 3, 7_000_000, rows * shards * units),
        name="feed_last" if last else "feed_first",
    )(*(scalars or ()), third, base, weights)


def body(
    latents, lengths, intersection, spatial_query, spatial_key, spatial_value, spatial_out,
    temporal_query, temporal_key, temporal_value, temporal_out, feed_value, feed_gate, feed_down,
):
    core = lax.axis_index("c")
    at = (lax.axis_index("zh") * lax.axis_size("x") + lax.axis_index("x")).astype(jnp.int32).reshape(1)
    units = feed_value.shape[1] // 2
    packed = jnp.stack([feed_value.T, feed_gate.T, feed_down.T])
    mine = lax.dynamic_slice_in_dim(packed, core * units, units, axis=1)
    gathered = lax.all_gather(mine, SPAN, axis=0, tiled=False)

    sent = pl.pallas_call(
        qkv_kernel,
        grid=(2,),
        in_specs=[pl.BlockSpec((HALF, PX, C), lambda i: (i, 0, 0))]
        + [pl.BlockSpec((C, C), lambda i: (0, 0))] * 3,
        out_specs=pl.BlockSpec((HEADS, HALF * PX, 256), lambda i: (i, 0, 0)),
        out_shape=jax.ShapeDtypeStruct((TOKS, HALF * PX, 256), BF16),
        compiler_params=params(),
        cost_estimate=cost(6 * FR * PX * C * C, 5_000_000),
        name="qkv",
    )(latents, spatial_query, spatial_key, spatial_value)
    got = lax.all_to_all(sent, TOK, 0, 0, tiled=True)
    context = pl.pallas_call(
        spatial_kernel,
        in_specs=vm(1),
        out_specs=pl.BlockSpec(memory_space=VMEM),
        out_shape=jax.ShapeDtypeStruct((TOKS, PX, 256), BF16),
        scratch_shapes=[pltpu.VMEM((TOKS * PX, 256), BF16)],
        compiler_params=params(),
        cost_estimate=cost(4 * 3 * 1024 * 1024 * 256, 2_000_000, 3 * 1024 * 1024),
        name="spatial",
    )(got)
    back = lax.all_to_all(context, TOK, 0, 0, tiled=True)
    middle, second, head, tail = pl.pallas_call(
        middle_kernel,
        in_specs=[pl.BlockSpec(memory_space=SMEM)] * 2 + vm(3),
        out_specs=[pl.BlockSpec(memory_space=VMEM)] * 4,
        out_shape=[
            jax.ShapeDtypeStruct((FR * PX, C), F32),
            jax.ShapeDtypeStruct((FR, PX, C), BF16),
            jax.ShapeDtypeStruct((OVL, PX, C), BF16),
            jax.ShapeDtypeStruct((OVL, PX, C), BF16),
        ],
        compiler_params=params(),
        cost_estimate=cost(2 * FR * PX * C * C, 4_000_000),
        name="middle",
    )(lengths, at, back, latents, spatial_out)
    count = lax.axis_size("zh") * lax.axis_size("x")
    prev = lax.ppermute(tail, SPAN, [(i, i + 1) for i in range(count - 1)])
    after = lax.ppermute(head, SPAN, [(i + 1, i) for i in range(count - 1)])
    tq, tk, tv = pl.pallas_call(
        time_kernel,
        in_specs=vm(4),
        out_specs=[pl.BlockSpec(memory_space=VMEM)] * 3,
        out_shape=[jax.ShapeDtypeStruct((FR, PX, C), BF16)] * 3,
        compiler_params=params(),
        cost_estimate=cost(6 * FR * PX * C * C, 4_500_000),
        name="time_qkv",
    )(second, temporal_query, temporal_key, temporal_value)
    window = FR + 2 * OVL
    late, third = pl.pallas_call(
        temporal_kernel,
        in_specs=[pl.BlockSpec(memory_space=SMEM)] * 3 + vm(9),
        out_specs=[pl.BlockSpec(memory_space=VMEM)] * 2,
        out_shape=[jax.ShapeDtypeStruct((FR * PX, C), F32), jax.ShapeDtypeStruct((FR * PX, C), BF16)],
        scratch_shapes=[
            pltpu.VMEM((window, PX, C), BF16),
            pltpu.VMEM((window, PX, C), BF16),
            pltpu.VMEM((FR, PX, C), BF16),
        ],
        compiler_params=params(),
        cost_estimate=cost(5_000_000_000, 8_000_000, 800_000),
        name="temporal",
    )(lengths, intersection, at, tq, tk, tv, prev, after, middle, temporal_key, temporal_value, temporal_out)
    other = lax.ppermute(gathered, "c", [(0, 1), (1, 0)])
    part = feed(third, late, gathered, None)
    refined = feed(third, part, other, (lengths, at))
    return refined.reshape(FR, PX, C)


def solution(mesh):
    fine = Mesh(mesh.devices.reshape(4, 4, 4, 2, 2), ("zh", "x", "y", "zl", "c"))
    token = P(SPAN, TOK, None)
    placed = (token,) + (P(),) * 10 + (P(None, SPAN),) * 3
    return jax.shard_map(body, mesh=fine, in_specs=placed, out_specs=token, check_vma=False)
```

```python
import functools

import jax
import jax.numpy as jnp
from jax import lax
from jax.experimental import pallas as pl
from jax.experimental.pallas import tpu as pltpu
from jax.sharding import Mesh
from jax.sharding import PartitionSpec as P

HEADS = 8
OVL = 4
HS = 80
C = 640
FR = 6
HALF = 3
PX = 64
TOKS = 16
PAIR = 16
F32 = jnp.float32
BF16 = jnp.bfloat16
CHUNK = 640
SPAN = ("zh", "x")
TOK = ("y", "zl", "c")
SCALE2 = HS ** (-0.5) * 1.4426950408889634
VMEM = pltpu.VMEM
SMEM = pltpu.SMEM
LAYOUT = ((80, 160, 0), (0, 160, 80), (0, 80, 160))


def params(mib=48):
    return pltpu.CompilerParams(vmem_limit_bytes=mib * 1024 * 1024)


def vm(n):
    return [pl.BlockSpec(memory_space=VMEM)] * n


def anys(n):
    return [pl.BlockSpec(memory_space=pl.ANY)] * n


def cost(flops, nbytes, exps=0):
    return pl.CostEstimate(flops=flops, bytes_accessed=nbytes, transcendentals=exps)


def dot(a, b):
    return jnp.dot(a, b, preferred_element_type=F32)


def dot_t(a, b):
    return lax.dot_general(a, b, (((1,), (1,)), ((), ())), preferred_element_type=F32)


def layer_norm(values):
    center = values - jnp.mean(values, axis=-1, keepdims=True)
    spread = jnp.mean(center * center, axis=-1, keepdims=True)
    return (center * lax.rsqrt(spread + 1e-05)).astype(BF16)


def lanes(shape, start, width):
    lane = lax.broadcasted_iota(jnp.int32, shape, len(shape) - 1)
    return (lane >= start) & (lane < start + width)


def qkv_kernel(x_ref, wq_ref, wk_ref, wv_ref, out_ref, x_s, w_s, o_s, sem, out_sem):
    loads = [pltpu.make_async_copy(x_ref.at[pl.ds(HALF * i, HALF)], x_s.at[i], sem.at[i]) for i in range(2)]
    loads += [pltpu.make_async_copy(w, w_s.at[i], sem.at[2 + i]) for i, w in enumerate((wq_ref, wk_ref, wv_ref))]
    for load in loads:
        load.start()
    stores = []
    pad = jnp.zeros((PX, 256 - 3 * HS), BF16)
    for half in range(2):
        loads[half].wait()
        normed = layer_norm(x_s[half].reshape(HALF * PX, C))
        qkv = []
        for i in range(3):
            if half == 0:
                loads[2 + i].wait()
            qkv.append(dot(normed, w_s[i]).astype(BF16))
        for h in range(HEADS):
            cols = slice(h * HS, (h + 1) * HS)
            for f in range(HALF):
                rows = slice(f * PX, (f + 1) * PX)
                order = sorted(zip(LAYOUT[f], qkv), key=lambda e: e[0])
                parts = [arr[rows, cols] for _, arr in order] + [pad]
                o_s[half * HEADS + h, rows, :] = jnp.concatenate(parts, axis=1)
        at = pl.ds(HEADS * half, HEADS)
        store = pltpu.make_async_copy(o_s.at[at], out_ref.at[at], out_sem.at[half])
        store.start()
        stores.append(store)
    for store in stores:
        store.wait()


def spatial_kernel(x_ref, out_ref, k_ref):
    n = TOKS * PX
    qb = 256
    dst = qb // PX
    for f in range(HALF):
        q_at, k_at, v_at = LAYOUT[f]
        rows = slice(f * PX, (f + 1) * PX)
        x = x_ref[:, rows, :].reshape(n, 256)
        k_ref[f] = pltpu.roll(x.astype(F32), (q_at - k_at) % 256, 1).astype(BF16)
        for i in range(n // qb):
            at = slice(i * dst, (i + 1) * dst)
            xq = x_ref[at, rows, :].reshape(qb, 256)
            xq = jnp.where(lanes((qb, 256), q_at, HS), xq, jnp.zeros_like(xq))
            s = dot_t(xq, k_ref[f])
            top = jnp.max(s, axis=-1, keepdims=True)
            e = jnp.exp2((s - top) * SCALE2)
            r = 1.0 / jnp.sum(e, axis=-1, keepdims=True)
            p = (e * r).astype(BF16)
            ctx = dot(p, x_ref[:, rows, :].reshape(n, 256)).astype(BF16)
            if f > 0:
                ctx = jnp.where(lanes((qb, 256), v_at, HS), ctx, out_ref[at].reshape(qb, 256))
            out_ref[at] = ctx.reshape(dst, PX, 256)


def middle_kernel(len_ref, at_ref, ctx_ref, x_ref, w_ref, mid_ref, second_ref, head_ref, tail_ref):
    rows = []
    for half in range(2):
        for f in range(HALF):
            cols = slice(f * HS, (f + 1) * HS)
            rows.append(jnp.concatenate([ctx_ref[half * HEADS + h, :, cols] for h in range(HEADS)], axis=1))
    context = jnp.concatenate(rows, axis=0)
    middle = x_ref[...].reshape(FR * PX, C) + dot(context, w_ref[...])
    mid_ref[...] = middle
    second = layer_norm(middle).reshape(FR, PX, C)
    second_ref[...] = second
    head_ref[...] = second[:OVL]
    own = len_ref[at_ref[0]]
    for j in range(OVL):
        at = jnp.maximum(own - OVL + j, 0)
        tail_ref[j] = second_ref[at]


def time_kernel(s_ref, wq_ref, wk_ref, wv_ref, q_ref, k_ref, v_ref):
    second = s_ref[...].reshape(FR * PX, C)
    q_ref[...] = dot(second, wq_ref[...]).astype(BF16).reshape(FR, PX, C)
    k_ref[...] = dot(second, wk_ref[...]).astype(BF16).reshape(FR, PX, C)
    v_ref[...] = dot(second, wv_ref[...]).astype(BF16).reshape(FR, PX, C)


def temporal_kernel(
    len_ref, inter_ref, at_ref, q_ref, k_ref, v_ref, prev_ref, next_ref, mid_ref, wk_ref, wv_ref, wo_ref,
    late_ref, third_ref, kw_ref, vw_ref, ctx_ref,
):
    me = at_ref[0]
    spans = len_ref.shape[0]
    own = len_ref[me]
    prev_len = len_ref[jnp.maximum(me - 1, 0)]
    next_len = len_ref[jnp.minimum(me + 1, spans - 1)]
    borrow = inter_ref[me]
    prev = prev_ref[...].reshape(OVL * PX, C)
    after = next_ref[...].reshape(OVL * PX, C)
    kw_ref[:OVL] = dot(prev, wk_ref[...]).astype(BF16).reshape(OVL, PX, C)
    kw_ref[OVL : OVL + FR] = k_ref[...]
    kw_ref[OVL + FR :] = dot(after, wk_ref[...]).astype(BF16).reshape(OVL, PX, C)
    vw_ref[:OVL] = dot(prev, wv_ref[...]).astype(BF16).reshape(OVL, PX, C)
    vw_ref[OVL : OVL + FR] = v_ref[...]
    vw_ref[OVL + FR :] = dot(after, wv_ref[...]).astype(BF16).reshape(OVL, PX, C)

    window = FR + 2 * OVL
    nrow, ncol = FR * PAIR, window * PAIR
    col = lax.broadcasted_iota(jnp.int32, (ncol, nrow), 0)
    row = lax.broadcasted_iota(jnp.int32, (ncol, nrow), 1)
    slot = col // PAIR
    low_prev = jnp.where(me > 0, jnp.maximum(OVL - borrow, OVL - prev_len), OVL)
    high_next = jnp.where(me < spans - 1, jnp.minimum(borrow, next_len), 0)
    live = ((slot >= low_prev) & (slot < OVL + own)) | ((slot >= OVL + FR) & (slot < OVL + FR + high_next))
    bias = jnp.where(live & ((col % PAIR) == (row % PAIR)), 0.0, -1e30)

    for g in range(PX // PAIR):
        at = slice(g * PAIR, (g + 1) * PAIR)
        qg = q_ref[:, at, :].reshape(nrow, C)
        kg = kw_ref[:, at, :].reshape(ncol, C)
        vg = vw_ref[:, at, :].reshape(ncol, C)
        acc = [jnp.zeros((nrow, 128), F32) for _ in range(C // 128)]
        for h in range(HEADS):
            t0, t1 = h * HS // 128, -(-(h + 1) * HS // 128)
            base, width = t0 * 128, (t1 - t0) * 128
            mask = lanes((nrow, width), h * HS - base, HS)
            qh = qg[:, base : base + width]
            qh = jnp.where(mask, qh, jnp.zeros_like(qh))
            s = dot_t(kg[:, base : base + width], qh) + bias
            top = jnp.max(s, axis=0, keepdims=True)
            e = jnp.exp2((s - top) * SCALE2)
            p = (e * (1.0 / jnp.sum(e, axis=0, keepdims=True))).astype(BF16)
            part = lax.dot_general(
                p, vg[:, base : base + width], (((0,), (0,)), ((), ())), preferred_element_type=F32
            )
            part = jnp.where(mask, part, 0.0)
            for t in range(t0, t1):
                acc[t] = acc[t] + part[:, (t - t0) * 128 : (t - t0 + 1) * 128]
        context = jnp.concatenate(acc, axis=1).astype(BF16)
        ctx_ref[:, at, :] = context.reshape(FR, PAIR, C)
    late = mid_ref[...] + dot(ctx_ref[...].reshape(FR * PX, C), wo_ref[...])
    late_ref[...] = late
    third_ref[...] = layer_norm(late)


def shift(x, axis, by):
    n = lax.axis_size(axis)
    return lax.ppermute(x, axis, [(i, (i + by) % n) for i in range(n)])


def swap(x, axis):
    n = lax.axis_size(axis)
    return lax.ppermute(x, axis, [(i, i ^ 1) for i in range(n)])


def spread_z(mine):
    part = jnp.concatenate([mine] + [shift(mine, "zh", by) for by in (1, -1, 2)], axis=1)
    return jnp.concatenate([part, swap(part, "y")], axis=1)


def after(x, *others):
    return lax.optimization_barrier((x, *others))[0]


def feed_kernel(first, count, *refs):
    if first:
        third_ref, base_ref, *refs = refs
    else:
        len_ref, at_ref, third_ref, base_ref, *refs = refs
    pieces = refs[:count]
    out_ref, w_ref, hid_ref, sems = refs[count:]
    loads, ends, end = [], [], 0
    for i, piece in enumerate(pieces):
        n = piece.shape[1]
        load = pltpu.make_async_copy(piece, w_ref.at[:, pl.ds(end, n)], sems.at[i])
        load.start()
        end += n
        loads.append(load)
        ends.append(end)
    third = third_ref[...]
    ready, there = 0, 0
    for start in range(0, end, CHUNK):
        while there < start + CHUNK:
            loads[ready].wait()
            there = ends[ready]
            ready += 1
        at = slice(start, start + CHUNK)
        gate = dot_t(third, w_ref[1, at])
        gate = 0.5 * gate * (1.0 + lax.erf(gate * (0.5**0.5)))
        hid_ref[:, at] = (dot_t(third, w_ref[0, at]) * gate).astype(BF16)
    total = base_ref[...] + dot(hid_ref[...], w_ref[2])
    if first:
        out_ref[...] = total
    else:
        row = lax.broadcasted_iota(jnp.int32, out_ref.shape, 0)
        out_ref[...] = jnp.where(row < len_ref[at_ref[0]] * PX, total, 0.0)


def feed(third, base, pieces, scalars):
    rows = FR * PX
    hidden = sum(p.shape[1] for p in pieces)
    count = len(pieces)
    return pl.pallas_call(
        functools.partial(feed_kernel, not scalars, count),
        in_specs=[pl.BlockSpec(memory_space=SMEM)] * len(scalars) + [pl.BlockSpec()] * 2 + anys(count),
        out_specs=pl.BlockSpec(),
        out_shape=jax.ShapeDtypeStruct((rows, C), F32),
        scratch_shapes=[
            pltpu.VMEM((3, hidden, C), BF16),
            pltpu.VMEM((rows, hidden), BF16),
            pltpu.SemaphoreType.DMA((count,)),
        ],
        compiler_params=params(32),
        cost_estimate=cost(2 * rows * C * hidden * 3, 7_000_000, rows * hidden),
        name="feed_last" if scalars else "feed_first",
    )(*scalars, third, base, *pieces)


def body(
    latents, lengths, intersection, spatial_query, spatial_key, spatial_value, spatial_out,
    temporal_query, temporal_key, temporal_value, temporal_out, feed_value, feed_gate, feed_down,
):
    core = lax.axis_index("c")
    at = (lax.axis_index("zh") * lax.axis_size("x") + lax.axis_index("x")).astype(jnp.int32).reshape(1)
    units = feed_value.shape[1] // 4
    packed = jnp.stack([feed_value.T, feed_gate.T, feed_down.T])
    mine = lax.dynamic_slice_in_dim(packed, (core * 2 + lax.axis_index("y") % 2) * units, units, axis=1)
    part = spread_z(mine)
    up, down = shift(part, "x", 1), shift(part, "x", -1)

    sent = pl.pallas_call(
        qkv_kernel,
        in_specs=anys(4),
        out_specs=pl.BlockSpec(memory_space=pl.ANY),
        out_shape=jax.ShapeDtypeStruct((TOKS, HALF * PX, 256), BF16),
        scratch_shapes=[
            pltpu.VMEM((2, HALF, PX, C), F32),
            pltpu.VMEM((3, C, C), BF16),
            pltpu.VMEM((TOKS, HALF * PX, 256), BF16),
            pltpu.SemaphoreType.DMA((5,)),
            pltpu.SemaphoreType.DMA((2,)),
        ],
        compiler_params=params(60),
        cost_estimate=cost(6 * FR * PX * C * C, 5_000_000),
        name="qkv",
    )(latents, spatial_query, spatial_key, spatial_value)
    got = lax.all_to_all(sent, TOK, 0, 0, tiled=True)
    context = pl.pallas_call(
        spatial_kernel,
        in_specs=vm(1),
        out_specs=pl.BlockSpec(),
        out_shape=jax.ShapeDtypeStruct((TOKS, PX, 256), BF16),
        scratch_shapes=[pltpu.VMEM((HALF, TOKS * PX, 256), BF16)],
        compiler_params=params(),
        cost_estimate=cost(4 * 3 * 1024 * 1024 * 256, 2_000_000, 3 * 1024 * 1024),
        name="spatial",
    )(got)
    back = lax.all_to_all(context, TOK, 0, 0, tiled=True)
    middle, second, head, tail = pl.pallas_call(
        middle_kernel,
        in_specs=[pl.BlockSpec(memory_space=SMEM)] * 2 + vm(3),
        out_specs=[pl.BlockSpec()] + [pl.BlockSpec(memory_space=VMEM)] * 3,
        out_shape=[
            jax.ShapeDtypeStruct((FR * PX, C), F32),
            jax.ShapeDtypeStruct((FR, PX, C), BF16),
            jax.ShapeDtypeStruct((OVL, PX, C), BF16),
            jax.ShapeDtypeStruct((OVL, PX, C), BF16),
        ],
        compiler_params=params(24),
        cost_estimate=cost(2 * FR * PX * C * C, 4_000_000),
        name="middle",
    )(lengths, at, back, latents, spatial_out)
    count = lax.axis_size("zh") * lax.axis_size("x")
    before = lax.ppermute(tail, SPAN, [(i, i + 1) for i in range(count - 1)])
    behind = lax.ppermute(head, SPAN, [(i + 1, i) for i in range(count - 1)])
    tq, tk, tv = pl.pallas_call(
        time_kernel,
        in_specs=vm(4),
        out_specs=[pl.BlockSpec(memory_space=VMEM)] * 3,
        out_shape=[jax.ShapeDtypeStruct((FR, PX, C), BF16)] * 3,
        compiler_params=params(16),
        cost_estimate=cost(6 * FR * PX * C * C, 4_500_000),
        name="time_qkv",
    )(second, temporal_query, temporal_key, temporal_value)
    half = part.shape[1] // 2
    near_up, near_down = after((up, down), second)
    up2, down2 = shift(near_up[:, :half], "x", 1), shift(near_down[:, half:], "x", -1)
    window = FR + 2 * OVL
    late, third = pl.pallas_call(
        temporal_kernel,
        in_specs=[pl.BlockSpec(memory_space=SMEM)] * 3 + vm(9),
        out_specs=[pl.BlockSpec()] * 2,
        out_shape=[jax.ShapeDtypeStruct((FR * PX, C), F32), jax.ShapeDtypeStruct((FR * PX, C), BF16)],
        scratch_shapes=[
            pltpu.VMEM((window, PX, C), BF16),
            pltpu.VMEM((window, PX, C), BF16),
            pltpu.VMEM((FR, PX, C), BF16),
        ],
        compiler_params=params(24),
        cost_estimate=cost(5_000_000_000, 8_000_000, 800_000),
        name="temporal",
    )(lengths, intersection, at, tq, tk, tv, before, behind, middle, temporal_key, temporal_value, temporal_out)
    far_up, far_down = after((up2, down2), third)
    own = (part, near_up, near_down, far_up, far_down)
    other = [swap(piece, "c") for piece in own]
    late = feed(third, late, own, ())
    refined = feed(third, late, other, (lengths, at))
    return refined.reshape(FR, PX, C)


def solution(mesh):
    fine = Mesh(mesh.devices.reshape(4, 4, 4, 2, 2), ("zh", "x", "y", "zl", "c"))
    token = P(SPAN, TOK, None)
    placed = (token,) + (P(),) * 10 + (P(None, SPAN),) * 3
    return jax.shard_map(body, mesh=fine, in_specs=placed, out_specs=token, check_vma=False)
```

```python
import functools

import jax
import jax.numpy as jnp
from jax import lax
from jax.experimental import pallas as pl
from jax.experimental.pallas import tpu as pltpu
from jax.sharding import Mesh
from jax.sharding import PartitionSpec as P

HEADS = 8
OVL = 4
HS = 80
C = 640
FR = 6
HALF = 3
PX = 64
TOKS = 16
PAIR = 16
F32 = jnp.float32
BF16 = jnp.bfloat16
CHUNK = 640
WINDOWS = ((0, (0, 1, 2)), (128, (3,)), (256, (4, 5)), (384, (6, 7)))
SPAN = ("zh", "x")
TOK = ("y", "zl", "c")
SCALE2 = HS ** (-0.5) * 1.4426950408889634
VMEM = pltpu.VMEM
SMEM = pltpu.SMEM
LAYOUT = ((80, 160, 0), (0, 160, 80), (0, 80, 160))


def params(mib=48):
    return pltpu.CompilerParams(vmem_limit_bytes=mib * 1024 * 1024)


def vm(n):
    return [pl.BlockSpec(memory_space=VMEM)] * n


def anys(n):
    return [pl.BlockSpec(memory_space=pl.ANY)] * n


QUICK = pl.CostEstimate(flops=1000, bytes_accessed=1000, transcendentals=0)


def dot(a, b):
    return jnp.dot(a, b, preferred_element_type=F32)


def dot_t(a, b):
    return lax.dot_general(a, b, (((1,), (1,)), ((), ())), preferred_element_type=F32)


def layer_norm(values):
    center = values - jnp.mean(values, axis=-1, keepdims=True)
    spread = jnp.mean(center * center, axis=-1, keepdims=True)
    return (center * lax.rsqrt(spread + 1e-05)).astype(BF16)


def lanes(shape, start, width):
    lane = lax.broadcasted_iota(jnp.int32, shape, len(shape) - 1)
    return (lane >= start) & (lane < start + width)


def qkv_kernel(x_ref, wq_ref, wk_ref, wv_ref, out_ref, x_s, w_s, o_s, sem, out_sem):
    loads = [pltpu.make_async_copy(x_ref.at[pl.ds(HALF * i, HALF)], x_s.at[i], sem.at[i]) for i in range(2)]
    loads += [pltpu.make_async_copy(w, w_s.at[i], sem.at[2 + i]) for i, w in enumerate((wq_ref, wk_ref, wv_ref))]
    for load in loads:
        load.start()
    stores = []
    pad = jnp.zeros((PX, 256 - 3 * HS), BF16)
    for half in range(2):
        loads[half].wait()
        normed = layer_norm(x_s[half].reshape(HALF * PX, C))
        qkv = []
        for i in range(3):
            if half == 0:
                loads[2 + i].wait()
            qkv.append(dot(normed, w_s[i]).astype(BF16))
        for h in range(HEADS):
            cols = slice(h * HS, (h + 1) * HS)
            for f in range(HALF):
                rows = slice(f * PX, (f + 1) * PX)
                order = sorted(zip(LAYOUT[f], qkv), key=lambda e: e[0])
                parts = [arr[rows, cols] for _, arr in order] + [pad]
                o_s[half * HEADS + h, rows, :] = jnp.concatenate(parts, axis=1)
        at = pl.ds(HEADS * half, HEADS)
        store = pltpu.make_async_copy(o_s.at[at], out_ref.at[at], out_sem.at[half])
        store.start()
        stores.append(store)
    for store in stores:
        store.wait()


def spatial_kernel(x_ref, out_ref, k_ref):
    n = TOKS * PX
    qb = 256
    dst = qb // PX
    for f in range(HALF):
        q_at, k_at, v_at = LAYOUT[f]
        rows = slice(f * PX, (f + 1) * PX)
        x = x_ref[:, rows, :].reshape(n, 256)
        k_ref[f] = pltpu.roll(x.astype(F32), (q_at - k_at) % 256, 1).astype(BF16)
        for i in range(n // qb):
            at = slice(i * dst, (i + 1) * dst)
            xq = x_ref[at, rows, :].reshape(qb, 256)
            xq = jnp.where(lanes((qb, 256), q_at, HS), xq, jnp.zeros_like(xq))
            s = dot_t(xq, k_ref[f])
            top = jnp.max(s, axis=-1, keepdims=True)
            e = jnp.exp2((s - top) * SCALE2)
            r = 1.0 / jnp.sum(e, axis=-1, keepdims=True)
            p = (e * r).astype(BF16)
            ctx = dot(p, x_ref[:, rows, :].reshape(n, 256)).astype(BF16)
            if f > 0:
                ctx = jnp.where(lanes((qb, 256), v_at, HS), ctx, out_ref[at].reshape(qb, 256))
            out_ref[at] = ctx.reshape(dst, PX, 256)


def middle_kernel(len_ref, at_ref, ctx_ref, x_ref, w_ref, mid_ref, second_ref, head_ref, tail_ref):
    rows = []
    for half in range(2):
        for f in range(HALF):
            cols = slice(f * HS, (f + 1) * HS)
            rows.append(jnp.concatenate([ctx_ref[half * HEADS + h, :, cols] for h in range(HEADS)], axis=1))
    context = jnp.concatenate(rows, axis=0)
    middle = x_ref[...].reshape(FR * PX, C) + dot(context, w_ref[...])
    mid_ref[...] = middle
    second = layer_norm(middle).reshape(FR, PX, C)
    second_ref[...] = second
    head_ref[...] = second[:OVL]
    own = len_ref[at_ref[0]]
    for j in range(OVL):
        at = jnp.maximum(own - OVL + j, 0)
        tail_ref[j] = second_ref[at]


def time_kernel(s_ref, wq_ref, wk_ref, wv_ref, q_ref, k_ref, v_ref):
    second = s_ref[...].reshape(FR * PX, C)
    q_ref[...] = dot(second, wq_ref[...]).astype(BF16).reshape(FR, PX, C)
    k_ref[...] = dot(second, wk_ref[...]).astype(BF16).reshape(FR, PX, C)
    v_ref[...] = dot(second, wv_ref[...]).astype(BF16).reshape(FR, PX, C)


def temporal_kernel(
    len_ref, inter_ref, at_ref, q_ref, k_ref, v_ref, prev_ref, next_ref, mid_ref, wk_ref, wv_ref, wo_ref,
    late_ref, third_ref, kw_ref, vw_ref, ctx_ref,
):
    me = at_ref[0]
    spans = len_ref.shape[0]
    own = len_ref[me]
    prev_len = len_ref[jnp.maximum(me - 1, 0)]
    next_len = len_ref[jnp.minimum(me + 1, spans - 1)]
    borrow = inter_ref[me]
    prev = prev_ref[...].reshape(OVL * PX, C)
    after = next_ref[...].reshape(OVL * PX, C)
    kw_ref[:OVL] = dot(prev, wk_ref[...]).astype(BF16).reshape(OVL, PX, C)
    kw_ref[OVL : OVL + FR] = k_ref[...]
    kw_ref[OVL + FR :] = dot(after, wk_ref[...]).astype(BF16).reshape(OVL, PX, C)
    vw_ref[:OVL] = dot(prev, wv_ref[...]).astype(BF16).reshape(OVL, PX, C)
    vw_ref[OVL : OVL + FR] = v_ref[...]
    vw_ref[OVL + FR :] = dot(after, wv_ref[...]).astype(BF16).reshape(OVL, PX, C)

    window = FR + 2 * OVL
    nrow, ncol = FR * PAIR, window * PAIR
    col = lax.broadcasted_iota(jnp.int32, (ncol, nrow), 0)
    row = lax.broadcasted_iota(jnp.int32, (ncol, nrow), 1)
    slot = col // PAIR
    low_prev = jnp.where(me > 0, jnp.maximum(OVL - borrow, OVL - prev_len), OVL)
    high_next = jnp.where(me < spans - 1, jnp.minimum(borrow, next_len), 0)
    live = ((slot >= low_prev) & (slot < OVL + own)) | ((slot >= OVL + FR) & (slot < OVL + FR + high_next))
    bias = jnp.where(live & ((col % PAIR) == (row % PAIR)), 0.0, -1e30)

    for g in range(PX // PAIR):
        at = slice(g * PAIR, (g + 1) * PAIR)
        qg = q_ref[:, at, :].reshape(nrow, C)
        kg = kw_ref[:, at, :].reshape(ncol, C)
        vg = vw_ref[:, at, :].reshape(ncol, C)
        acc = [None] * (C // 128)
        for base, heads in WINDOWS:
            cols = slice(base, base + 256)
            masks = [lanes((nrow, 256), h * HS - base, HS) for h in heads]
            qw = qg[:, cols]
            qs = jnp.concatenate([jnp.where(m, qw, jnp.zeros_like(qw)) for m in masks], axis=0)
            s = dot_t(kg[:, cols], qs) + jnp.concatenate([bias] * len(heads), axis=1)
            top = jnp.max(s, axis=0, keepdims=True)
            e = jnp.exp2((s - top) * SCALE2)
            p = (e * (1.0 / jnp.sum(e, axis=0, keepdims=True))).astype(BF16)
            part = lax.dot_general(p, vg[:, cols], (((0,), (0,)), ((), ())), preferred_element_type=F32)
            merged = None
            for i, m in enumerate(masks):
                one = part[i * nrow : (i + 1) * nrow]
                merged = jnp.where(m, one, 0.0 if merged is None else merged)
            for t in range(2):
                piece = merged[:, t * 128 : (t + 1) * 128]
                i = base // 128 + t
                acc[i] = piece if acc[i] is None else acc[i] + piece
        context = jnp.concatenate(acc, axis=1).astype(BF16)
        ctx_ref[:, at, :] = context.reshape(FR, PAIR, C)
    late = mid_ref[...] + dot(ctx_ref[...].reshape(FR * PX, C), wo_ref[...])
    late_ref[...] = late
    third_ref[...] = layer_norm(late)


def shift(x, axis, by):
    n = lax.axis_size(axis)
    return lax.ppermute(x, axis, [(i, (i + by) % n) for i in range(n)])


def swap(x, axis):
    n = lax.axis_size(axis)
    return lax.ppermute(x, axis, [(i, i ^ 1) for i in range(n)])


def step_z(x):
    n = lax.axis_size("zh")
    pairs = [(2 * k + 1, (2 * k + 2) % (2 * n)) for k in range(n)]
    pairs += [(2 * k, (2 * k - 1) % (2 * n)) for k in range(n)]
    return lax.ppermute(x, ("zh", "zl"), pairs)


def after(x, *others):
    return lax.optimization_barrier((x, *others))[0]


def feed_kernel(first, count, *refs):
    if first:
        third_ref, base_ref, *refs = refs
    else:
        len_ref, at_ref, third_ref, base_ref, *refs = refs
    pieces = refs[:count]
    out_ref, w_ref, hid_ref, sems = refs[count:]
    loads, ends, end = [], [], 0
    for i, piece in enumerate(pieces):
        n = piece.shape[1]
        load = pltpu.make_async_copy(piece, w_ref.at[:, pl.ds(end, n)], sems.at[i])
        load.start()
        end += n
        loads.append(load)
        ends.append(end)
    third = third_ref[...]
    ready, there = 0, 0
    for start in range(0, end, CHUNK):
        while there < start + CHUNK:
            loads[ready].wait()
            there = ends[ready]
            ready += 1
        at = slice(start, start + CHUNK)
        gate = dot_t(third, w_ref[1, at])
        gate = 0.5 * gate * (1.0 + lax.erf(gate * (0.5**0.5)))
        hid_ref[:, at] = (dot_t(third, w_ref[0, at]) * gate).astype(BF16)
    total = base_ref[...] + dot(hid_ref[...], w_ref[2])
    if first:
        out_ref[...] = total
    else:
        row = lax.broadcasted_iota(jnp.int32, out_ref.shape, 0)
        out_ref[...] = jnp.where(row < len_ref[at_ref[0]] * PX, total, 0.0)


def feed(third, base, pieces, scalars):
    rows = FR * PX
    hidden = sum(p.shape[1] for p in pieces)
    count = len(pieces)
    return pl.pallas_call(
        functools.partial(feed_kernel, not scalars, count),
        in_specs=[pl.BlockSpec(memory_space=SMEM)] * len(scalars) + [pl.BlockSpec()] * 2 + anys(count),
        out_specs=pl.BlockSpec(),
        out_shape=jax.ShapeDtypeStruct((rows, C), F32),
        scratch_shapes=[
            pltpu.VMEM((3, hidden, C), BF16),
            pltpu.VMEM((rows, hidden), BF16),
            pltpu.SemaphoreType.DMA((count,)),
        ],
        compiler_params=params(32),
        cost_estimate=QUICK,
        name="feed_last" if scalars else "feed_first",
    )(*scalars, third, base, *pieces)


def body(
    latents, lengths, intersection, spatial_query, spatial_key, spatial_value, spatial_out,
    temporal_query, temporal_key, temporal_value, temporal_out, feed_value, feed_gate, feed_down,
):
    core = lax.axis_index("c")
    at = (lax.axis_index("zh") * lax.axis_size("x") + lax.axis_index("x")).astype(jnp.int32).reshape(1)
    units = feed_value.shape[1] // 2
    packed = jnp.stack([feed_value.T, feed_gate.T, feed_down.T])
    mine = lax.dynamic_slice_in_dim(packed, core * units, units, axis=1)
    level = lax.axis_index("zl")
    next_1 = step_z(mine)
    next_2 = swap(next_1, "zl")
    part = jnp.concatenate([mine, next_1], axis=1)
    part_up, part_down = shift(part, "x", 1), shift(part, "x", -1)
    far_up = shift(part_up, "x", 1)

    sent = pl.pallas_call(
        qkv_kernel,
        in_specs=anys(4),
        out_specs=pl.BlockSpec(memory_space=pl.ANY),
        out_shape=jax.ShapeDtypeStruct((TOKS, HALF * PX, 256), BF16),
        scratch_shapes=[
            pltpu.VMEM((2, HALF, PX, C), F32),
            pltpu.VMEM((3, C, C), BF16),
            pltpu.VMEM((TOKS, HALF * PX, 256), BF16),
            pltpu.SemaphoreType.DMA((5,)),
            pltpu.SemaphoreType.DMA((2,)),
        ],
        compiler_params=params(60),
        cost_estimate=QUICK,
        name="qkv",
    )(latents, spatial_query, spatial_key, spatial_value)
    got = lax.all_to_all(sent, TOK, 0, 0, tiled=True)
    got, part, next_2 = lax.optimization_barrier((got, part, next_2))
    half = units // 2
    next_3 = step_z(lax.dynamic_slice_in_dim(next_2, (1 - level) * half, half, axis=1))
    context = pl.pallas_call(
        spatial_kernel,
        in_specs=vm(1),
        out_specs=pl.BlockSpec(),
        out_shape=jax.ShapeDtypeStruct((TOKS, PX, 256), BF16),
        scratch_shapes=[pltpu.VMEM((HALF, TOKS * PX, 256), BF16)],
        compiler_params=params(),
        cost_estimate=QUICK,
        name="spatial",
    )(got)
    context, next_3 = lax.optimization_barrier((context, next_3))
    back = lax.all_to_all(context, TOK, 0, 0, tiled=True)
    next_4 = swap(next_3, "zl")
    pair = jnp.concatenate([next_2, next_3, next_4], axis=1)
    pair_up, pair_down = shift(pair, "x", 1), shift(pair, "x", -1)
    far_down = shift(pair_down, "x", -1)
    first = [swap(piece, "c") for piece in (part, part_up, part_down)]
    back, pair, *first = lax.optimization_barrier((back, pair, *first))
    middle, second, head, tail = pl.pallas_call(
        middle_kernel,
        in_specs=[pl.BlockSpec(memory_space=SMEM)] * 2 + vm(3),
        out_specs=[pl.BlockSpec()] + [pl.BlockSpec(memory_space=VMEM)] * 3,
        out_shape=[
            jax.ShapeDtypeStruct((FR * PX, C), F32),
            jax.ShapeDtypeStruct((FR, PX, C), BF16),
            jax.ShapeDtypeStruct((OVL, PX, C), BF16),
            jax.ShapeDtypeStruct((OVL, PX, C), BF16),
        ],
        compiler_params=params(24),
        cost_estimate=QUICK,
        name="middle",
    )(lengths, at, back, latents, spatial_out)
    count = lax.axis_size("zh") * lax.axis_size("x")
    before = lax.ppermute(tail, SPAN, [(i, i + 1) for i in range(count - 1)])
    behind = lax.ppermute(head, SPAN, [(i + 1, i) for i in range(count - 1)])
    tq, tk, tv = pl.pallas_call(
        time_kernel,
        in_specs=vm(4),
        out_specs=[pl.BlockSpec(memory_space=VMEM)] * 3,
        out_shape=[jax.ShapeDtypeStruct((FR, PX, C), BF16)] * 3,
        compiler_params=params(16),
        cost_estimate=QUICK,
        name="time_qkv",
    )(second, temporal_query, temporal_key, temporal_value)
    tq, pair_up, pair_down, far_up = lax.optimization_barrier((tq, pair_up, pair_down, far_up))
    window = FR + 2 * OVL
    late, third = pl.pallas_call(
        temporal_kernel,
        in_specs=[pl.BlockSpec(memory_space=SMEM)] * 3 + vm(9),
        out_specs=[pl.BlockSpec()] * 2,
        out_shape=[jax.ShapeDtypeStruct((FR * PX, C), F32), jax.ShapeDtypeStruct((FR * PX, C), BF16)],
        scratch_shapes=[
            pltpu.VMEM((window, PX, C), BF16),
            pltpu.VMEM((window, PX, C), BF16),
            pltpu.VMEM((FR, PX, C), BF16),
        ],
        compiler_params=params(24),
        cost_estimate=QUICK,
        name="temporal",
    )(lengths, intersection, at, tq, tk, tv, before, behind, middle, temporal_key, temporal_value, temporal_out)
    own = (part, part_up, part_down, pair, pair_up, pair_down, far_up, far_down)
    other = first + [swap(piece, "c") for piece in own[3:]]
    late = feed(third, late, own, ())
    refined = feed(third, late, other, (lengths, at))
    return refined.reshape(FR, PX, C)


def solution(mesh):
    fine = Mesh(mesh.devices.reshape(4, 4, 4, 2, 2), ("zh", "x", "y", "zl", "c"))
    token = P(SPAN, TOK, None)
    placed = (token,) + (P(),) * 10 + (P(None, SPAN),) * 3
    return jax.shard_map(body, mesh=fine, in_specs=placed, out_specs=token, check_vma=False)
```

```python
import functools

import jax
import jax.numpy as jnp
from jax import lax
from jax.experimental import pallas as pl
from jax.experimental.pallas import tpu as pltpu
from jax.sharding import Mesh
from jax.sharding import PartitionSpec as P

HEADS = 8
OVL = 4
HS = 80
C = 640
FR = 6
HALF = 3
PX = 64
TOKS = 16
PAIR = 16
F32 = jnp.float32
BF16 = jnp.bfloat16
CHUNK = 256
WINDOWS = ((0, (0, 1, 2)), (128, (3,)), (256, (4, 5)), (384, (6, 7)))
SPAN = ("zh", "x")
TOK = ("y", "zl", "c")
SCALE2 = HS ** (-0.5) * 1.4426950408889634
VMEM = pltpu.VMEM
SMEM = pltpu.SMEM
LAYOUT = ((80, 160, 0), (0, 160, 80), (0, 80, 160))


def params(mib=48):
    return pltpu.CompilerParams(vmem_limit_bytes=mib * 1024 * 1024)


def vm(n):
    return [pl.BlockSpec(memory_space=VMEM)] * n


def anys(n):
    return [pl.BlockSpec(memory_space=pl.ANY)] * n


SLOW = pl.CostEstimate(flops=20_000_000_000, bytes_accessed=10_000_000, transcendentals=0)
QUICK = pl.CostEstimate(flops=1000, bytes_accessed=1000, transcendentals=0)


def dot(a, b):
    return jnp.dot(a, b, preferred_element_type=F32)


def dot_t(a, b):
    return lax.dot_general(a, b, (((1,), (1,)), ((), ())), preferred_element_type=F32)


def layer_norm(values):
    center = values - jnp.mean(values, axis=-1, keepdims=True)
    spread = jnp.mean(center * center, axis=-1, keepdims=True)
    return (center * lax.rsqrt(spread + 1e-05)).astype(BF16)


def lanes(shape, start, width):
    lane = lax.broadcasted_iota(jnp.int32, shape, len(shape) - 1)
    return (lane >= start) & (lane < start + width)


def qkv_kernel(x_ref, wq_ref, wk_ref, wv_ref, out_ref, x_s, w_s, o_s, sem, out_sem):
    loads = [pltpu.make_async_copy(x_ref.at[pl.ds(HALF * i, HALF)], x_s.at[i], sem.at[i]) for i in range(2)]
    loads += [pltpu.make_async_copy(w, w_s.at[i], sem.at[2 + i]) for i, w in enumerate((wq_ref, wk_ref, wv_ref))]
    for load in loads:
        load.start()
    stores = []
    pad = jnp.zeros((PX, 256 - 3 * HS), BF16)
    for half in range(2):
        loads[half].wait()
        normed = layer_norm(x_s[half].reshape(HALF * PX, C))
        qkv = []
        for i in range(3):
            if half == 0:
                loads[2 + i].wait()
            qkv.append(dot(normed, w_s[i]).astype(BF16))
        for h in range(HEADS):
            cols = slice(h * HS, (h + 1) * HS)
            for f in range(HALF):
                rows = slice(f * PX, (f + 1) * PX)
                order = sorted(zip(LAYOUT[f], qkv), key=lambda e: e[0])
                parts = [arr[rows, cols] for _, arr in order] + [pad]
                o_s[half * HEADS + h, rows, :] = jnp.concatenate(parts, axis=1)
        at = pl.ds(HEADS * half, HEADS)
        store = pltpu.make_async_copy(o_s.at[at], out_ref.at[at], out_sem.at[half])
        store.start()
        stores.append(store)
    for store in stores:
        store.wait()


def spatial_kernel(x_ref, out_ref, k_ref):
    n = TOKS * PX
    qb = 256
    dst = qb // PX
    for f in range(HALF):
        q_at, k_at, v_at = LAYOUT[f]
        rows = slice(f * PX, (f + 1) * PX)
        x = x_ref[:, rows, :].reshape(n, 256)
        k_ref[f] = pltpu.roll(x.astype(F32), (q_at - k_at) % 256, 1).astype(BF16)
        for i in range(n // qb):
            at = slice(i * dst, (i + 1) * dst)
            xq = x_ref[at, rows, :].reshape(qb, 256)
            xq = jnp.where(lanes((qb, 256), q_at, HS), xq, jnp.zeros_like(xq))
            s = dot_t(xq, k_ref[f])
            top = jnp.max(s, axis=-1, keepdims=True)
            e = jnp.exp2((s - top) * SCALE2)
            r = 1.0 / jnp.sum(e, axis=-1, keepdims=True)
            p = (e * r).astype(BF16)
            ctx = dot(p, x_ref[:, rows, :].reshape(n, 256)).astype(BF16)
            if f > 0:
                ctx = jnp.where(lanes((qb, 256), v_at, HS), ctx, out_ref[at].reshape(qb, 256))
            out_ref[at] = ctx.reshape(dst, PX, 256)


def middle_kernel(len_ref, at_ref, ctx_ref, x_ref, w_ref, mid_ref, second_ref, head_ref, tail_ref):
    rows = []
    for half in range(2):
        for f in range(HALF):
            cols = slice(f * HS, (f + 1) * HS)
            rows.append(jnp.concatenate([ctx_ref[half * HEADS + h, :, cols] for h in range(HEADS)], axis=1))
    context = jnp.concatenate(rows, axis=0)
    middle = x_ref[...].reshape(FR * PX, C) + dot(context, w_ref[...])
    mid_ref[...] = middle
    second = layer_norm(middle).reshape(FR, PX, C)
    second_ref[...] = second
    head_ref[...] = second[:OVL]
    own = len_ref[at_ref[0]]
    for j in range(OVL):
        at = jnp.maximum(own - OVL + j, 0)
        tail_ref[j] = second_ref[at]


def time_kernel(s_ref, wq_ref, wk_ref, wv_ref, q_ref, k_ref, v_ref):
    second = s_ref[...].reshape(FR * PX, C)
    q_ref[...] = dot(second, wq_ref[...]).astype(BF16).reshape(FR, PX, C)
    k_ref[...] = dot(second, wk_ref[...]).astype(BF16).reshape(FR, PX, C)
    v_ref[...] = dot(second, wv_ref[...]).astype(BF16).reshape(FR, PX, C)


def temporal_kernel(
    len_ref, inter_ref, at_ref, q_ref, k_ref, v_ref, prev_ref, next_ref, mid_ref, wk_ref, wv_ref, wo_ref,
    late_ref, third_ref, kw_ref, vw_ref, ctx_ref,
):
    me = at_ref[0]
    spans = len_ref.shape[0]
    own = len_ref[me]
    prev_len = len_ref[jnp.maximum(me - 1, 0)]
    next_len = len_ref[jnp.minimum(me + 1, spans - 1)]
    borrow = inter_ref[me]
    prev = prev_ref[...].reshape(OVL * PX, C)
    after = next_ref[...].reshape(OVL * PX, C)
    kw_ref[:OVL] = dot(prev, wk_ref[...]).astype(BF16).reshape(OVL, PX, C)
    kw_ref[OVL : OVL + FR] = k_ref[...]
    kw_ref[OVL + FR :] = dot(after, wk_ref[...]).astype(BF16).reshape(OVL, PX, C)
    vw_ref[:OVL] = dot(prev, wv_ref[...]).astype(BF16).reshape(OVL, PX, C)
    vw_ref[OVL : OVL + FR] = v_ref[...]
    vw_ref[OVL + FR :] = dot(after, wv_ref[...]).astype(BF16).reshape(OVL, PX, C)

    window = FR + 2 * OVL
    nrow, ncol = FR * PAIR, window * PAIR
    col = lax.broadcasted_iota(jnp.int32, (ncol, nrow), 0)
    row = lax.broadcasted_iota(jnp.int32, (ncol, nrow), 1)
    slot = col // PAIR
    low_prev = jnp.where(me > 0, jnp.maximum(OVL - borrow, OVL - prev_len), OVL)
    high_next = jnp.where(me < spans - 1, jnp.minimum(borrow, next_len), 0)
    live = ((slot >= low_prev) & (slot < OVL + own)) | ((slot >= OVL + FR) & (slot < OVL + FR + high_next))
    bias = jnp.where(live & ((col % PAIR) == (row % PAIR)), 0.0, -1e30)

    for g in range(PX // PAIR):
        at = slice(g * PAIR, (g + 1) * PAIR)
        qg = q_ref[:, at, :].reshape(nrow, C)
        kg = kw_ref[:, at, :].reshape(ncol, C)
        vg = vw_ref[:, at, :].reshape(ncol, C)
        acc = [None] * (C // 128)
        for base, heads in WINDOWS:
            cols = slice(base, base + 256)
            masks = [lanes((nrow, 256), h * HS - base, HS) for h in heads]
            qw = qg[:, cols]
            qs = jnp.concatenate([jnp.where(m, qw, jnp.zeros_like(qw)) for m in masks], axis=0)
            s = dot_t(kg[:, cols], qs) + jnp.concatenate([bias] * len(heads), axis=1)
            top = jnp.max(s, axis=0, keepdims=True)
            e = jnp.exp2((s - top) * SCALE2)
            p = (e * (1.0 / jnp.sum(e, axis=0, keepdims=True))).astype(BF16)
            part = lax.dot_general(p, vg[:, cols], (((0,), (0,)), ((), ())), preferred_element_type=F32)
            merged = None
            for i, m in enumerate(masks):
                one = part[i * nrow : (i + 1) * nrow]
                merged = jnp.where(m, one, 0.0 if merged is None else merged)
            for t in range(2):
                piece = merged[:, t * 128 : (t + 1) * 128]
                i = base // 128 + t
                acc[i] = piece if acc[i] is None else acc[i] + piece
        context = jnp.concatenate(acc, axis=1).astype(BF16)
        ctx_ref[:, at, :] = context.reshape(FR, PAIR, C)
    late = mid_ref[...] + dot(ctx_ref[...].reshape(FR * PX, C), wo_ref[...])
    late_ref[...] = late
    third_ref[...] = layer_norm(late)


def shift(x, axis, by):
    n = lax.axis_size(axis)
    return lax.ppermute(x, axis, [(i, (i + by) % n) for i in range(n)])


def swap(x, axis):
    n = lax.axis_size(axis)
    return lax.ppermute(x, axis, [(i, i ^ 1) for i in range(n)])


def step_z(x):
    n = lax.axis_size("zh")
    pairs = [(2 * k + 1, (2 * k + 2) % (2 * n)) for k in range(n)]
    pairs += [(2 * k, (2 * k - 1) % (2 * n)) for k in range(n)]
    return lax.ppermute(x, ("zh", "zl"), pairs)


def after(x, *others):
    return lax.optimization_barrier((x, *others))[0]


def feed_kernel(count, last, *refs):
    if last:
        len_ref, at_ref, *refs = refs
    third_ref, base_ref, *refs = refs
    pieces = refs[:count]
    out_ref, w_ref, hid_ref, sems = refs[count:]
    loads, ends, end = [], [], 0
    for i, piece in enumerate(pieces):
        n = piece.shape[1]
        load = pltpu.make_async_copy(piece, w_ref.at[:, pl.ds(end, n)], sems.at[i])
        load.start()
        end += n
        loads.append(load)
        ends.append(end)
    third = third_ref[...]
    ready, there = 0, 0
    for start in range(0, end, CHUNK):
        stop = min(start + CHUNK, end)
        while there < stop:
            loads[ready].wait()
            there = ends[ready]
            ready += 1
        at = slice(start, stop)
        gate = dot_t(third, w_ref[1, at])
        gate = 0.5 * gate * (1.0 + lax.erf(gate * (0.5**0.5)))
        hid_ref[:, at] = (dot_t(third, w_ref[0, at]) * gate).astype(BF16)
    total = base_ref[...] + dot(hid_ref[...], w_ref[2])
    if last:
        row = lax.broadcasted_iota(jnp.int32, out_ref.shape, 0)
        total = jnp.where(row < len_ref[at_ref[0]] * PX, total, 0.0)
    out_ref[...] = total


def feed(third, base, pieces, scalars):
    rows = FR * PX
    hidden = sum(p.shape[1] for p in pieces)
    count = len(pieces)
    return pl.pallas_call(
        functools.partial(feed_kernel, count, bool(scalars)),
        in_specs=[pl.BlockSpec(memory_space=SMEM)] * len(scalars) + [pl.BlockSpec()] * 2 + anys(count),
        out_specs=pl.BlockSpec(),
        out_shape=jax.ShapeDtypeStruct((rows, C), F32),
        scratch_shapes=[
            pltpu.VMEM((3, hidden, C), BF16),
            pltpu.VMEM((rows, hidden), BF16),
            pltpu.SemaphoreType.DMA((count,)),
        ],
        compiler_params=params(40),
        cost_estimate=SLOW,
        name="feed_last" if scalars else "feed_first",
    )(*scalars, third, base, *pieces)


def body(
    latents, lengths, intersection, spatial_query, spatial_key, spatial_value, spatial_out,
    temporal_query, temporal_key, temporal_value, temporal_out, feed_value, feed_gate, feed_down,
):
    core = lax.axis_index("c")
    at = (lax.axis_index("zh") * lax.axis_size("x") + lax.axis_index("x")).astype(jnp.int32).reshape(1)
    units = feed_value.shape[1] // 2
    packed = jnp.stack([feed_value.T, feed_gate.T, feed_down.T])
    mine = lax.dynamic_slice_in_dim(packed, core * units, units, axis=1)
    level = lax.axis_index("zl")
    next_1 = step_z(mine)
    next_2 = swap(next_1, "zl")
    part = jnp.concatenate([mine, next_1], axis=1)
    part_up, part_down = shift(part, "x", 1), shift(part, "x", -1)
    far_up = shift(part_up, "x", 1)

    sent = pl.pallas_call(
        qkv_kernel,
        in_specs=anys(4),
        out_specs=pl.BlockSpec(memory_space=pl.ANY),
        out_shape=jax.ShapeDtypeStruct((TOKS, HALF * PX, 256), BF16),
        scratch_shapes=[
            pltpu.VMEM((2, HALF, PX, C), F32),
            pltpu.VMEM((3, C, C), BF16),
            pltpu.VMEM((TOKS, HALF * PX, 256), BF16),
            pltpu.SemaphoreType.DMA((5,)),
            pltpu.SemaphoreType.DMA((2,)),
        ],
        compiler_params=params(60),
        cost_estimate=QUICK,
        name="qkv",
    )(latents, spatial_query, spatial_key, spatial_value)
    got = lax.all_to_all(sent, TOK, 0, 0, tiled=True)
    got, part, next_2 = lax.optimization_barrier((got, part, next_2))
    half = units // 2
    next_3 = step_z(lax.dynamic_slice_in_dim(next_2, (1 - level) * half, half, axis=1))
    context = pl.pallas_call(
        spatial_kernel,
        in_specs=vm(1),
        out_specs=pl.BlockSpec(),
        out_shape=jax.ShapeDtypeStruct((TOKS, PX, 256), BF16),
        scratch_shapes=[pltpu.VMEM((HALF, TOKS * PX, 256), BF16)],
        compiler_params=params(),
        cost_estimate=QUICK,
        name="spatial",
    )(got)
    context, next_3 = lax.optimization_barrier((context, next_3))
    back = lax.all_to_all(context, TOK, 0, 0, tiled=True)
    next_4 = swap(next_3, "zl")
    pair = jnp.concatenate([next_2, next_3, next_4], axis=1)
    pair_up, pair_down = shift(pair, "x", 1), shift(pair, "x", -1)
    first = [swap(piece, "c") for piece in (part, part_up, part_down)]
    back, *first = lax.optimization_barrier((back, *first))
    middle, second, head, tail = pl.pallas_call(
        middle_kernel,
        in_specs=[pl.BlockSpec(memory_space=SMEM)] * 2 + vm(3),
        out_specs=[pl.BlockSpec()] + [pl.BlockSpec(memory_space=VMEM)] * 3,
        out_shape=[
            jax.ShapeDtypeStruct((FR * PX, C), F32),
            jax.ShapeDtypeStruct((FR, PX, C), BF16),
            jax.ShapeDtypeStruct((OVL, PX, C), BF16),
            jax.ShapeDtypeStruct((OVL, PX, C), BF16),
        ],
        compiler_params=params(24),
        cost_estimate=QUICK,
        name="middle",
    )(lengths, at, back, latents, spatial_out)
    head, tail, far_up = lax.optimization_barrier((head, tail, far_up))
    count = lax.axis_size("zh") * lax.axis_size("x")
    before = lax.ppermute(tail, SPAN, [(i, i + 1) for i in range(count - 1)])
    behind = lax.ppermute(head, SPAN, [(i + 1, i) for i in range(count - 1)])
    tq, tk, tv = pl.pallas_call(
        time_kernel,
        in_specs=vm(4),
        out_specs=[pl.BlockSpec(memory_space=VMEM)] * 3,
        out_shape=[jax.ShapeDtypeStruct((FR, PX, C), BF16)] * 3,
        compiler_params=params(16),
        cost_estimate=QUICK,
        name="time_qkv",
    )(second, temporal_query, temporal_key, temporal_value)
    half = pair.shape[1] // 2
    ends = (pair_up[:, :half], pair_down[:, half:])
    before, behind, tq, *ends = lax.optimization_barrier((before, behind, tq, *ends))
    far = [shift(ends[0], "x", 1), shift(ends[1], "x", -1)]
    window = FR + 2 * OVL
    late, third = pl.pallas_call(
        temporal_kernel,
        in_specs=[pl.BlockSpec(memory_space=SMEM)] * 3 + vm(9),
        out_specs=[pl.BlockSpec()] * 2,
        out_shape=[jax.ShapeDtypeStruct((FR * PX, C), F32), jax.ShapeDtypeStruct((FR * PX, C), BF16)],
        scratch_shapes=[
            pltpu.VMEM((window, PX, C), BF16),
            pltpu.VMEM((window, PX, C), BF16),
            pltpu.VMEM((FR, PX, C), BF16),
        ],
        compiler_params=params(24),
        cost_estimate=SLOW,
        name="temporal",
    )(lengths, intersection, at, tq, tk, tv, before, behind, middle, temporal_key, temporal_value, temporal_out)
    late_own = after((pair, pair_up, pair_down, far_up), third)
    late_other = [swap(piece, "c") for piece in late_own]
    far = list(after(tuple(far), third))
    far += [swap(piece, "c") for piece in far]
    late = feed(third, late, [part, part_up, part_down, *first, *late_own], ())
    refined = feed(third, late, [*late_other, *far], (lengths, at))
    return refined.reshape(FR, PX, C)


def solution(mesh):
    fine = Mesh(mesh.devices.reshape(4, 4, 4, 2, 2), ("zh", "x", "y", "zl", "c"))
    token = P(SPAN, TOK, None)
    placed = (token,) + (P(),) * 10 + (P(None, SPAN),) * 3
    return jax.shard_map(body, mesh=fine, in_specs=placed, out_specs=token, check_vma=False)
```

```python
import functools

import jax
import jax.numpy as jnp
from jax import lax
from jax.experimental import pallas as pl
from jax.experimental.pallas import tpu as pltpu
from jax.sharding import Mesh
from jax.sharding import PartitionSpec as P

HEADS = 8
OVL = 4
HS = 80
C = 640
FR = 6
HALF = 3
PX = 64
TOKS = 16
PAIR = 16
F32 = jnp.float32
BF16 = jnp.bfloat16
CHUNK = 256
WINDOWS = ((0, (0, 1, 2)), (128, (3,)), (256, (4, 5)), (384, (6, 7)))
SPAN = ("zh", "x")
TOK = ("y", "zl", "c")
SCALE2 = HS ** (-0.5) * 1.4426950408889634
VMEM = pltpu.VMEM
SMEM = pltpu.SMEM
LAYOUT = ((80, 160, 0), (0, 160, 80), (0, 80, 160))


def params(mib=48):
    return pltpu.CompilerParams(vmem_limit_bytes=mib * 1024 * 1024)


def vm(n):
    return [pl.BlockSpec(memory_space=VMEM)] * n


def anys(n):
    return [pl.BlockSpec(memory_space=pl.ANY)] * n


SLOW = pl.CostEstimate(flops=20_000_000_000, bytes_accessed=10_000_000, transcendentals=0)
QUICK = pl.CostEstimate(flops=1000, bytes_accessed=1000, transcendentals=0)


def dot(a, b):
    return jnp.dot(a, b, preferred_element_type=F32)


def dot_t(a, b):
    return lax.dot_general(a, b, (((1,), (1,)), ((), ())), preferred_element_type=F32)


def layer_norm(values):
    center = values - jnp.mean(values, axis=-1, keepdims=True)
    spread = jnp.mean(center * center, axis=-1, keepdims=True)
    return (center * lax.rsqrt(spread + 1e-05)).astype(BF16)


def lanes(shape, start, width):
    lane = lax.broadcasted_iota(jnp.int32, shape, len(shape) - 1)
    return (lane >= start) & (lane < start + width)


def qkv_kernel(x_ref, wq_ref, wk_ref, wv_ref, out_ref, x_s, w_s, o_s, sem, out_sem):
    loads = [pltpu.make_async_copy(x_ref.at[pl.ds(HALF * i, HALF)], x_s.at[i], sem.at[i]) for i in range(2)]
    loads += [pltpu.make_async_copy(w, w_s.at[i], sem.at[2 + i]) for i, w in enumerate((wq_ref, wk_ref, wv_ref))]
    for load in loads:
        load.start()
    stores = []
    pad = jnp.zeros((PX, 256 - 3 * HS), BF16)
    for half in range(2):
        loads[half].wait()
        normed = layer_norm(x_s[half].reshape(HALF * PX, C))
        qkv = []
        for i in range(3):
            if half == 0:
                loads[2 + i].wait()
            qkv.append(dot(normed, w_s[i]).astype(BF16))
        for h in range(HEADS):
            cols = slice(h * HS, (h + 1) * HS)
            for f in range(HALF):
                rows = slice(f * PX, (f + 1) * PX)
                order = sorted(zip(LAYOUT[f], qkv), key=lambda e: e[0])
                parts = [arr[rows, cols] for _, arr in order] + [pad]
                o_s[half * HEADS + h, rows, :] = jnp.concatenate(parts, axis=1)
        at = pl.ds(HEADS * half, HEADS)
        store = pltpu.make_async_copy(o_s.at[at], out_ref.at[at], out_sem.at[half])
        store.start()
        stores.append(store)
    for store in stores:
        store.wait()


def spatial_kernel(x_ref, out_ref, k_ref):
    n = TOKS * PX
    qb = 256
    dst = qb // PX
    for f in range(HALF):
        q_at, k_at, v_at = LAYOUT[f]
        rows = slice(f * PX, (f + 1) * PX)
        x = x_ref[:, rows, :].reshape(n, 256)
        k_ref[f] = pltpu.roll(x.astype(F32), (q_at - k_at) % 256, 1).astype(BF16)
        for i in range(n // qb):
            at = slice(i * dst, (i + 1) * dst)
            xq = x_ref[at, rows, :].reshape(qb, 256)
            xq = jnp.where(lanes((qb, 256), q_at, HS), xq, jnp.zeros_like(xq))
            s = dot_t(xq, k_ref[f])
            top = jnp.max(s, axis=-1, keepdims=True)
            e = jnp.exp2((s - top) * SCALE2)
            r = 1.0 / jnp.sum(e, axis=-1, keepdims=True)
            p = (e * r).astype(BF16)
            ctx = dot(p, x_ref[:, rows, :].reshape(n, 256)).astype(BF16)
            if f > 0:
                ctx = jnp.where(lanes((qb, 256), v_at, HS), ctx, out_ref[at].reshape(qb, 256))
            out_ref[at] = ctx.reshape(dst, PX, 256)


def middle_kernel(len_ref, at_ref, ctx_ref, x_ref, w_ref, mid_ref, second_ref, head_ref, tail_ref):
    rows = []
    for half in range(2):
        for f in range(HALF):
            cols = slice(f * HS, (f + 1) * HS)
            rows.append(jnp.concatenate([ctx_ref[half * HEADS + h, :, cols] for h in range(HEADS)], axis=1))
    context = jnp.concatenate(rows, axis=0)
    middle = x_ref[...].reshape(FR * PX, C) + dot(context, w_ref[...])
    mid_ref[...] = middle
    second = layer_norm(middle).reshape(FR, PX, C)
    second_ref[...] = second
    head_ref[...] = second[:OVL]
    own = len_ref[at_ref[0]]
    for j in range(OVL):
        at = jnp.maximum(own - OVL + j, 0)
        tail_ref[j] = second_ref[at]


def time_kernel(s_ref, wq_ref, wk_ref, wv_ref, q_ref, k_ref, v_ref):
    second = s_ref[...].reshape(FR * PX, C)
    q_ref[...] = dot(second, wq_ref[...]).astype(BF16).reshape(FR, PX, C)
    k_ref[...] = dot(second, wk_ref[...]).astype(BF16).reshape(FR, PX, C)
    v_ref[...] = dot(second, wv_ref[...]).astype(BF16).reshape(FR, PX, C)


def temporal_kernel(
    len_ref, inter_ref, at_ref, q_ref, k_ref, v_ref, prev_ref, next_ref, mid_ref, wk_ref, wv_ref, wo_ref,
    late_ref, third_ref, kw_ref, vw_ref, ctx_ref,
):
    me = at_ref[0]
    spans = len_ref.shape[0]
    own = len_ref[me]
    prev_len = len_ref[jnp.maximum(me - 1, 0)]
    next_len = len_ref[jnp.minimum(me + 1, spans - 1)]
    borrow = inter_ref[me]
    prev = prev_ref[...].reshape(OVL * PX, C)
    after = next_ref[...].reshape(OVL * PX, C)
    kw_ref[:OVL] = dot(prev, wk_ref[...]).astype(BF16).reshape(OVL, PX, C)
    kw_ref[OVL : OVL + FR] = k_ref[...]
    kw_ref[OVL + FR :] = dot(after, wk_ref[...]).astype(BF16).reshape(OVL, PX, C)
    vw_ref[:OVL] = dot(prev, wv_ref[...]).astype(BF16).reshape(OVL, PX, C)
    vw_ref[OVL : OVL + FR] = v_ref[...]
    vw_ref[OVL + FR :] = dot(after, wv_ref[...]).astype(BF16).reshape(OVL, PX, C)

    window = FR + 2 * OVL
    nrow, ncol = FR * PAIR, window * PAIR
    col = lax.broadcasted_iota(jnp.int32, (ncol, nrow), 0)
    row = lax.broadcasted_iota(jnp.int32, (ncol, nrow), 1)
    slot = col // PAIR
    low_prev = jnp.where(me > 0, jnp.maximum(OVL - borrow, OVL - prev_len), OVL)
    high_next = jnp.where(me < spans - 1, jnp.minimum(borrow, next_len), 0)
    live = ((slot >= low_prev) & (slot < OVL + own)) | ((slot >= OVL + FR) & (slot < OVL + FR + high_next))
    bias = jnp.where(live & ((col % PAIR) == (row % PAIR)), 0.0, -1e30)

    for g in range(PX // PAIR):
        at = slice(g * PAIR, (g + 1) * PAIR)
        qg = q_ref[:, at, :].reshape(nrow, C)
        kg = kw_ref[:, at, :].reshape(ncol, C)
        vg = vw_ref[:, at, :].reshape(ncol, C)
        acc = [None] * (C // 128)
        for base, heads in WINDOWS:
            cols = slice(base, base + 256)
            masks = [lanes((nrow, 256), h * HS - base, HS) for h in heads]
            qw = qg[:, cols]
            qs = jnp.concatenate([jnp.where(m, qw, jnp.zeros_like(qw)) for m in masks], axis=0)
            s = dot_t(kg[:, cols], qs) + jnp.concatenate([bias] * len(heads), axis=1)
            top = jnp.max(s, axis=0, keepdims=True)
            e = jnp.exp2((s - top) * SCALE2)
            p = (e * (1.0 / jnp.sum(e, axis=0, keepdims=True))).astype(BF16)
            part = lax.dot_general(p, vg[:, cols], (((0,), (0,)), ((), ())), preferred_element_type=F32)
            merged = None
            for i, m in enumerate(masks):
                one = part[i * nrow : (i + 1) * nrow]
                merged = jnp.where(m, one, 0.0 if merged is None else merged)
            for t in range(2):
                piece = merged[:, t * 128 : (t + 1) * 128]
                i = base // 128 + t
                acc[i] = piece if acc[i] is None else acc[i] + piece
        context = jnp.concatenate(acc, axis=1).astype(BF16)
        ctx_ref[:, at, :] = context.reshape(FR, PAIR, C)
    late = mid_ref[...] + dot(ctx_ref[...].reshape(FR * PX, C), wo_ref[...])
    late_ref[...] = late
    third_ref[...] = layer_norm(late)


def shift(x, axis, by):
    n = lax.axis_size(axis)
    return lax.ppermute(x, axis, [(i, (i + by) % n) for i in range(n)])


def swap(x, axis):
    n = lax.axis_size(axis)
    return lax.ppermute(x, axis, [(i, i ^ 1) for i in range(n)])


def step_z(x):
    n = lax.axis_size("zh")
    pairs = [(2 * k + 1, (2 * k + 2) % (2 * n)) for k in range(n)]
    pairs += [(2 * k, (2 * k - 1) % (2 * n)) for k in range(n)]
    return lax.ppermute(x, ("zh", "zl"), pairs)


def after(x, *others):
    return lax.optimization_barrier((x, *others))[0]


def feed_kernel(count, last, *refs):
    if last:
        len_ref, at_ref, *refs = refs
    third_ref, base_ref, *refs = refs
    pieces = refs[:count]
    out_ref, w_ref, hid_ref, sems = refs[count:]
    loads, ends, end = [], [], 0
    for i, piece in enumerate(pieces):
        n = piece.shape[1]
        load = pltpu.make_async_copy(piece, w_ref.at[:, pl.ds(end, n)], sems.at[i])
        load.start()
        end += n
        loads.append(load)
        ends.append(end)
    third = third_ref[...]
    ready, there = 0, 0
    for start in range(0, end, CHUNK):
        stop = min(start + CHUNK, end)
        while there < stop:
            loads[ready].wait()
            there = ends[ready]
            ready += 1
        at = slice(start, stop)
        gate = dot_t(third, w_ref[1, at])
        gate = 0.5 * gate * (1.0 + lax.erf(gate * (0.5**0.5)))
        hid_ref[:, at] = (dot_t(third, w_ref[0, at]) * gate).astype(BF16)
    total = base_ref[...] + dot(hid_ref[...], w_ref[2])
    if last:
        row = lax.broadcasted_iota(jnp.int32, out_ref.shape, 0)
        total = jnp.where(row < len_ref[at_ref[0]] * PX, total, 0.0)
    out_ref[...] = total


def feed(third, base, pieces, scalars):
    rows = FR * PX
    hidden = sum(p.shape[1] for p in pieces)
    count = len(pieces)
    return pl.pallas_call(
        functools.partial(feed_kernel, count, bool(scalars)),
        in_specs=[pl.BlockSpec(memory_space=SMEM)] * len(scalars) + [pl.BlockSpec()] * 2 + anys(count),
        out_specs=pl.BlockSpec(),
        out_shape=jax.ShapeDtypeStruct((rows, C), F32),
        scratch_shapes=[
            pltpu.VMEM((3, hidden, C), BF16),
            pltpu.VMEM((rows, hidden), BF16),
            pltpu.SemaphoreType.DMA((count,)),
        ],
        compiler_params=params(40),
        cost_estimate=SLOW,
        name="feed_last" if scalars else "feed_first",
    )(*scalars, third, base, *pieces)


def body(
    latents, lengths, intersection, spatial_query, spatial_key, spatial_value, spatial_out,
    temporal_query, temporal_key, temporal_value, temporal_out, feed_value, feed_gate, feed_down,
):
    core = lax.axis_index("c")
    at = (lax.axis_index("zh") * lax.axis_size("x") + lax.axis_index("x")).astype(jnp.int32).reshape(1)
    units = feed_value.shape[1] // 2
    packed = jnp.stack([feed_value.T, feed_gate.T, feed_down.T])
    mine = lax.dynamic_slice_in_dim(packed, core * units, units, axis=1)
    level = lax.axis_index("zl")
    next_1 = step_z(mine)
    part = jnp.concatenate([mine, next_1], axis=1)
    part_up, part_down = shift(part, "x", 1), shift(part, "x", -1)
    far_up = shift(part_up, "x", 1)

    sent = pl.pallas_call(
        qkv_kernel,
        in_specs=anys(4),
        out_specs=pl.BlockSpec(memory_space=pl.ANY),
        out_shape=jax.ShapeDtypeStruct((TOKS, HALF * PX, 256), BF16),
        scratch_shapes=[
            pltpu.VMEM((2, HALF, PX, C), F32),
            pltpu.VMEM((3, C, C), BF16),
            pltpu.VMEM((TOKS, HALF * PX, 256), BF16),
            pltpu.SemaphoreType.DMA((5,)),
            pltpu.SemaphoreType.DMA((2,)),
        ],
        compiler_params=params(60),
        cost_estimate=QUICK,
        name="qkv",
    )(latents, spatial_query, spatial_key, spatial_value)
    got = lax.all_to_all(sent, TOK, 0, 0, tiled=True)
    got, part = lax.optimization_barrier((got, part))
    next_2 = swap(after(next_1, got), "zl")
    half = units // 2
    next_3 = step_z(lax.dynamic_slice_in_dim(next_2, (1 - level) * half, half, axis=1))
    context = pl.pallas_call(
        spatial_kernel,
        in_specs=vm(1),
        out_specs=pl.BlockSpec(),
        out_shape=jax.ShapeDtypeStruct((TOKS, PX, 256), BF16),
        scratch_shapes=[pltpu.VMEM((HALF, TOKS * PX, 256), BF16)],
        compiler_params=params(),
        cost_estimate=QUICK,
        name="spatial",
    )(got)
    back = lax.all_to_all(context, TOK, 0, 0, tiled=True)
    next_4 = swap(next_3, "zl")
    pair = jnp.concatenate([next_2, next_3, next_4], axis=1)
    pair_up, pair_down = shift(pair, "x", 1), shift(pair, "x", -1)
    first = [swap(piece, "c") for piece in (part, part_up, part_down)]
    back, *first = lax.optimization_barrier((back, *first))
    middle, second, head, tail = pl.pallas_call(
        middle_kernel,
        in_specs=[pl.BlockSpec(memory_space=SMEM)] * 2 + vm(3),
        out_specs=[pl.BlockSpec()] + [pl.BlockSpec(memory_space=VMEM)] * 3,
        out_shape=[
            jax.ShapeDtypeStruct((FR * PX, C), F32),
            jax.ShapeDtypeStruct((FR, PX, C), BF16),
            jax.ShapeDtypeStruct((OVL, PX, C), BF16),
            jax.ShapeDtypeStruct((OVL, PX, C), BF16),
        ],
        compiler_params=params(24),
        cost_estimate=QUICK,
        name="middle",
    )(lengths, at, back, latents, spatial_out)
    head, tail, far_up = lax.optimization_barrier((head, tail, far_up))
    count = lax.axis_size("zh") * lax.axis_size("x")
    before = lax.ppermute(tail, SPAN, [(i, i + 1) for i in range(count - 1)])
    behind = lax.ppermute(head, SPAN, [(i + 1, i) for i in range(count - 1)])
    tq, tk, tv = pl.pallas_call(
        time_kernel,
        in_specs=vm(4),
        out_specs=[pl.BlockSpec(memory_space=VMEM)] * 3,
        out_shape=[jax.ShapeDtypeStruct((FR, PX, C), BF16)] * 3,
        compiler_params=params(16),
        cost_estimate=QUICK,
        name="time_qkv",
    )(second, temporal_query, temporal_key, temporal_value)
    half = pair.shape[1] // 2
    ends = (pair_up[:, :half], pair_down[:, half:])
    before, behind, tq, *ends = lax.optimization_barrier((before, behind, tq, *ends))
    far = [shift(ends[0], "x", 1), shift(ends[1], "x", -1)]
    window = FR + 2 * OVL
    late, third = pl.pallas_call(
        temporal_kernel,
        in_specs=[pl.BlockSpec(memory_space=SMEM)] * 3 + vm(9),
        out_specs=[pl.BlockSpec()] * 2,
        out_shape=[jax.ShapeDtypeStruct((FR * PX, C), F32), jax.ShapeDtypeStruct((FR * PX, C), BF16)],
        scratch_shapes=[
            pltpu.VMEM((window, PX, C), BF16),
            pltpu.VMEM((window, PX, C), BF16),
            pltpu.VMEM((FR, PX, C), BF16),
        ],
        compiler_params=params(24),
        cost_estimate=SLOW,
        name="temporal",
    )(lengths, intersection, at, tq, tk, tv, before, behind, middle, temporal_key, temporal_value, temporal_out)
    late_own = after((pair, pair_up, pair_down, far_up), third)
    late_other = [swap(piece, "c") for piece in late_own]
    far = list(after(tuple(far), third))
    far += [swap(piece, "c") for piece in far]
    late = feed(third, late, [part, part_up, part_down, *first, *late_own], ())
    refined = feed(third, late, [*late_other, *far], (lengths, at))
    return refined.reshape(FR, PX, C)


def solution(mesh):
    fine = Mesh(mesh.devices.reshape(4, 4, 4, 2, 2), ("zh", "x", "y", "zl", "c"))
    token = P(SPAN, TOK, None)
    placed = (token,) + (P(),) * 10 + (P(None, SPAN),) * 3
    return jax.shard_map(body, mesh=fine, in_specs=placed, out_specs=token, check_vma=False)
```

```python
import functools

import jax
import jax.numpy as jnp
from jax import lax
from jax.experimental import pallas as pl
from jax.experimental.pallas import tpu as pltpu
from jax.sharding import Mesh
from jax.sharding import PartitionSpec as P

HEADS = 8
OVL = 4
HS = 80
C = 640
FR = 6
HALF = 3
PX = 64
TOKS = 16
PAIR = 16
F32 = jnp.float32
BF16 = jnp.bfloat16
CHUNK = 256
WINDOWS = ((0, (0, 1, 2)), (128, (3,)), (256, (4, 5)), (384, (6, 7)))
SPAN = ("zh", "x")
TOK = ("y", "zl", "c")
SCALE2 = HS ** (-0.5) * 1.4426950408889634
VMEM = pltpu.VMEM
SMEM = pltpu.SMEM
LAYOUT = ((80, 160, 0), (0, 160, 80), (0, 80, 160))


def params(mib=48):
    return pltpu.CompilerParams(vmem_limit_bytes=mib * 1024 * 1024)


def vm(n):
    return [pl.BlockSpec(memory_space=VMEM)] * n


def anys(n):
    return [pl.BlockSpec(memory_space=pl.ANY)] * n


SLOW = pl.CostEstimate(flops=20_000_000_000, bytes_accessed=10_000_000, transcendentals=0)
QUICK = pl.CostEstimate(flops=1000, bytes_accessed=1000, transcendentals=0)


def dot(a, b):
    return jnp.dot(a, b, preferred_element_type=F32)


def dot_t(a, b):
    return lax.dot_general(a, b, (((1,), (1,)), ((), ())), preferred_element_type=F32)


def layer_norm(values):
    center = values - jnp.mean(values, axis=-1, keepdims=True)
    spread = jnp.mean(center * center, axis=-1, keepdims=True)
    return (center * lax.rsqrt(spread + 1e-05)).astype(BF16)


def lanes(shape, start, width):
    lane = lax.broadcasted_iota(jnp.int32, shape, len(shape) - 1)
    return (lane >= start) & (lane < start + width)


def qkv_kernel(x_ref, wq_ref, wk_ref, wv_ref, out_ref, x_s, w_s, o_s, sem, out_sem):
    loads = [pltpu.make_async_copy(x_ref.at[pl.ds(HALF * i, HALF)], x_s.at[i], sem.at[i]) for i in range(2)]
    loads += [pltpu.make_async_copy(w, w_s.at[i], sem.at[2 + i]) for i, w in enumerate((wq_ref, wk_ref, wv_ref))]
    for load in loads:
        load.start()
    stores = []
    pad = jnp.zeros((PX, 256 - 3 * HS), BF16)
    for half in range(2):
        loads[half].wait()
        normed = layer_norm(x_s[half].reshape(HALF * PX, C))
        qkv = []
        for i in range(3):
            if half == 0:
                loads[2 + i].wait()
            qkv.append(dot(normed, w_s[i]).astype(BF16))
        for h in range(HEADS):
            cols = slice(h * HS, (h + 1) * HS)
            for f in range(HALF):
                rows = slice(f * PX, (f + 1) * PX)
                order = sorted(zip(LAYOUT[f], qkv), key=lambda e: e[0])
                parts = [arr[rows, cols] for _, arr in order] + [pad]
                o_s[half * HEADS + h, rows, :] = jnp.concatenate(parts, axis=1)
        at = pl.ds(HEADS * half, HEADS)
        store = pltpu.make_async_copy(o_s.at[at], out_ref.at[at], out_sem.at[half])
        store.start()
        stores.append(store)
    for store in stores:
        store.wait()


def spatial_kernel(x_ref, out_ref, k_ref):
    n = TOKS * PX
    qb = 256
    dst = qb // PX
    for f in range(HALF):
        q_at, k_at, v_at = LAYOUT[f]
        rows = slice(f * PX, (f + 1) * PX)
        x = x_ref[:, rows, :].reshape(n, 256)
        k_ref[f] = pltpu.roll(x.astype(F32), (q_at - k_at) % 256, 1).astype(BF16)
        for i in range(n // qb):
            at = slice(i * dst, (i + 1) * dst)
            xq = x_ref[at, rows, :].reshape(qb, 256)
            xq = jnp.where(lanes((qb, 256), q_at, HS), xq, jnp.zeros_like(xq))
            s = dot_t(xq, k_ref[f])
            top = jnp.max(s, axis=-1, keepdims=True)
            e = jnp.exp2((s - top) * SCALE2)
            r = 1.0 / jnp.sum(e, axis=-1, keepdims=True)
            p = (e * r).astype(BF16)
            ctx = dot(p, x_ref[:, rows, :].reshape(n, 256)).astype(BF16)
            if f > 0:
                ctx = jnp.where(lanes((qb, 256), v_at, HS), ctx, out_ref[at].reshape(qb, 256))
            out_ref[at] = ctx.reshape(dst, PX, 256)


def middle_kernel(len_ref, at_ref, ctx_ref, x_ref, w_ref, mid_ref, second_ref, head_ref, tail_ref):
    rows = []
    for half in range(2):
        for f in range(HALF):
            cols = slice(f * HS, (f + 1) * HS)
            rows.append(jnp.concatenate([ctx_ref[half * HEADS + h, :, cols] for h in range(HEADS)], axis=1))
    context = jnp.concatenate(rows, axis=0)
    middle = x_ref[...].reshape(FR * PX, C) + dot(context, w_ref[...])
    mid_ref[...] = middle
    second = layer_norm(middle).reshape(FR, PX, C)
    second_ref[...] = second
    head_ref[...] = second[:OVL]
    own = len_ref[at_ref[0]]
    for j in range(OVL):
        at = jnp.maximum(own - OVL + j, 0)
        tail_ref[j] = second_ref[at]


def time_kernel(s_ref, wq_ref, wk_ref, wv_ref, q_ref, k_ref, v_ref):
    second = s_ref[...].reshape(FR * PX, C)
    q_ref[...] = dot(second, wq_ref[...]).astype(BF16).reshape(FR, PX, C)
    k_ref[...] = dot(second, wk_ref[...]).astype(BF16).reshape(FR, PX, C)
    v_ref[...] = dot(second, wv_ref[...]).astype(BF16).reshape(FR, PX, C)


def temporal_kernel(
    len_ref, inter_ref, at_ref, q_ref, k_ref, v_ref, prev_ref, next_ref, mid_ref, wk_ref, wv_ref, wo_ref,
    late_ref, third_ref, kw_ref, vw_ref, ctx_ref,
):
    me = at_ref[0]
    spans = len_ref.shape[0]
    own = len_ref[me]
    prev_len = len_ref[jnp.maximum(me - 1, 0)]
    next_len = len_ref[jnp.minimum(me + 1, spans - 1)]
    borrow = inter_ref[me]
    prev = prev_ref[...].reshape(OVL * PX, C)
    after = next_ref[...].reshape(OVL * PX, C)
    kw_ref[:OVL] = dot(prev, wk_ref[...]).astype(BF16).reshape(OVL, PX, C)
    kw_ref[OVL : OVL + FR] = k_ref[...]
    kw_ref[OVL + FR :] = dot(after, wk_ref[...]).astype(BF16).reshape(OVL, PX, C)
    vw_ref[:OVL] = dot(prev, wv_ref[...]).astype(BF16).reshape(OVL, PX, C)
    vw_ref[OVL : OVL + FR] = v_ref[...]
    vw_ref[OVL + FR :] = dot(after, wv_ref[...]).astype(BF16).reshape(OVL, PX, C)

    window = FR + 2 * OVL
    nrow, ncol = FR * PAIR, window * PAIR
    col = lax.broadcasted_iota(jnp.int32, (ncol, nrow), 0)
    row = lax.broadcasted_iota(jnp.int32, (ncol, nrow), 1)
    slot = col // PAIR
    low_prev = jnp.where(me > 0, jnp.maximum(OVL - borrow, OVL - prev_len), OVL)
    high_next = jnp.where(me < spans - 1, jnp.minimum(borrow, next_len), 0)
    live = ((slot >= low_prev) & (slot < OVL + own)) | ((slot >= OVL + FR) & (slot < OVL + FR + high_next))
    bias = jnp.where(live & ((col % PAIR) == (row % PAIR)), 0.0, -1e30)

    for g in range(PX // PAIR):
        at = slice(g * PAIR, (g + 1) * PAIR)
        qg = q_ref[:, at, :].reshape(nrow, C)
        kg = kw_ref[:, at, :].reshape(ncol, C)
        vg = vw_ref[:, at, :].reshape(ncol, C)
        acc = [None] * (C // 128)
        for base, heads in WINDOWS:
            cols = slice(base, base + 256)
            masks = [lanes((nrow, 256), h * HS - base, HS) for h in heads]
            qw = qg[:, cols]
            qs = jnp.concatenate([jnp.where(m, qw, jnp.zeros_like(qw)) for m in masks], axis=0)
            s = dot_t(kg[:, cols], qs) + jnp.concatenate([bias] * len(heads), axis=1)
            top = jnp.max(s, axis=0, keepdims=True)
            e = jnp.exp2((s - top) * SCALE2)
            p = (e * (1.0 / jnp.sum(e, axis=0, keepdims=True))).astype(BF16)
            part = lax.dot_general(p, vg[:, cols], (((0,), (0,)), ((), ())), preferred_element_type=F32)
            merged = None
            for i, m in enumerate(masks):
                one = part[i * nrow : (i + 1) * nrow]
                merged = jnp.where(m, one, 0.0 if merged is None else merged)
            for t in range(2):
                piece = merged[:, t * 128 : (t + 1) * 128]
                i = base // 128 + t
                acc[i] = piece if acc[i] is None else acc[i] + piece
        context = jnp.concatenate(acc, axis=1).astype(BF16)
        ctx_ref[:, at, :] = context.reshape(FR, PAIR, C)
    late = mid_ref[...] + dot(ctx_ref[...].reshape(FR * PX, C), wo_ref[...])
    late_ref[...] = late
    third_ref[...] = layer_norm(late)


def shift(x, axis, by):
    n = lax.axis_size(axis)
    return lax.ppermute(x, axis, [(i, (i + by) % n) for i in range(n)])


def swap(x, axis):
    n = lax.axis_size(axis)
    return lax.ppermute(x, axis, [(i, i ^ 1) for i in range(n)])


def step_z(x):
    n = lax.axis_size("zh")
    pairs = [(2 * k + 1, (2 * k + 2) % (2 * n)) for k in range(n)]
    pairs += [(2 * k, (2 * k - 1) % (2 * n)) for k in range(n)]
    return lax.ppermute(x, ("zh", "zl"), pairs)


def after(x, *others):
    return lax.optimization_barrier((x, *others))[0]


def feed_kernel(count, last, *refs):
    if last:
        len_ref, at_ref, *refs = refs
    third_ref, base_ref, *refs = refs
    pieces = refs[:count]
    out_ref, w_ref, hid_ref, sems = refs[count:]
    loads, ends, end = [], [], 0
    for i, piece in enumerate(pieces):
        n = piece.shape[1]
        load = pltpu.make_async_copy(piece, w_ref.at[:, pl.ds(end, n)], sems.at[i])
        load.start()
        end += n
        loads.append(load)
        ends.append(end)
    third = third_ref[...]
    ready, there = 0, 0
    for start in range(0, end, CHUNK):
        stop = min(start + CHUNK, end)
        while there < stop:
            loads[ready].wait()
            there = ends[ready]
            ready += 1
        at = slice(start, stop)
        gate = dot_t(third, w_ref[1, at])
        gate = 0.5 * gate * (1.0 + lax.erf(gate * (0.5**0.5)))
        hid_ref[:, at] = (dot_t(third, w_ref[0, at]) * gate).astype(BF16)
    total = base_ref[...] + dot(hid_ref[...], w_ref[2])
    if last:
        row = lax.broadcasted_iota(jnp.int32, out_ref.shape, 0)
        total = jnp.where(row < len_ref[at_ref[0]] * PX, total, 0.0)
    out_ref[...] = total


def feed(third, base, pieces, scalars):
    rows = FR * PX
    hidden = sum(p.shape[1] for p in pieces)
    count = len(pieces)
    return pl.pallas_call(
        functools.partial(feed_kernel, count, bool(scalars)),
        in_specs=[pl.BlockSpec(memory_space=SMEM)] * len(scalars) + [pl.BlockSpec()] * 2 + anys(count),
        out_specs=pl.BlockSpec(),
        out_shape=jax.ShapeDtypeStruct((rows, C), F32),
        scratch_shapes=[
            pltpu.VMEM((3, hidden, C), BF16),
            pltpu.VMEM((rows, hidden), BF16),
            pltpu.SemaphoreType.DMA((count,)),
        ],
        compiler_params=params(40),
        cost_estimate=SLOW,
        name="feed_last" if scalars else "feed_first",
    )(*scalars, third, base, *pieces)


def body(
    latents, lengths, intersection, spatial_query, spatial_key, spatial_value, spatial_out,
    temporal_query, temporal_key, temporal_value, temporal_out, feed_value, feed_gate, feed_down,
):
    core = lax.axis_index("c")
    at = (lax.axis_index("zh") * lax.axis_size("x") + lax.axis_index("x")).astype(jnp.int32).reshape(1)
    units = feed_value.shape[1] // 2
    packed = jnp.stack([feed_value.T, feed_gate.T, feed_down.T])
    mine = lax.dynamic_slice_in_dim(packed, core * units, units, axis=1)
    level = lax.axis_index("zl")
    next_1 = step_z(mine)
    part = jnp.concatenate([mine, next_1], axis=1)
    part_up, part_down = shift(part, "x", 1), shift(part, "x", -1)
    far_up = shift(part_up, "x", 1)

    sent = pl.pallas_call(
        qkv_kernel,
        in_specs=anys(4),
        out_specs=pl.BlockSpec(memory_space=pl.ANY),
        out_shape=jax.ShapeDtypeStruct((TOKS, HALF * PX, 256), BF16),
        scratch_shapes=[
            pltpu.VMEM((2, HALF, PX, C), F32),
            pltpu.VMEM((3, C, C), BF16),
            pltpu.VMEM((TOKS, HALF * PX, 256), BF16),
            pltpu.SemaphoreType.DMA((5,)),
            pltpu.SemaphoreType.DMA((2,)),
        ],
        compiler_params=params(60),
        cost_estimate=QUICK,
        name="qkv",
    )(latents, spatial_query, spatial_key, spatial_value)
    got = lax.all_to_all(sent, TOK, 0, 0, tiled=True)
    got, part = lax.optimization_barrier((got, part))
    next_2 = swap(after(next_1, got), "zl")
    half = units // 2
    next_3 = step_z(lax.dynamic_slice_in_dim(next_2, (1 - level) * half, half, axis=1))
    context = pl.pallas_call(
        spatial_kernel,
        in_specs=vm(1),
        out_specs=pl.BlockSpec(),
        out_shape=jax.ShapeDtypeStruct((TOKS, PX, 256), BF16),
        scratch_shapes=[pltpu.VMEM((HALF, TOKS * PX, 256), BF16)],
        compiler_params=params(28),
        cost_estimate=QUICK,
        name="spatial",
    )(got)
    back = lax.all_to_all(context, TOK, 0, 0, tiled=True)
    next_4 = swap(next_3, "zl")
    pair = jnp.concatenate([next_2, next_3, next_4], axis=1)
    pair_up, pair_down = shift(pair, "x", 1), shift(pair, "x", -1)
    first = [swap(piece, "c") for piece in (part, part_up, part_down)]
    back, *first = lax.optimization_barrier((back, *first))
    middle, second, head, tail = pl.pallas_call(
        middle_kernel,
        in_specs=[pl.BlockSpec(memory_space=SMEM)] * 2 + vm(3),
        out_specs=[pl.BlockSpec()] + [pl.BlockSpec(memory_space=VMEM)] * 3,
        out_shape=[
            jax.ShapeDtypeStruct((FR * PX, C), F32),
            jax.ShapeDtypeStruct((FR, PX, C), BF16),
            jax.ShapeDtypeStruct((OVL, PX, C), BF16),
            jax.ShapeDtypeStruct((OVL, PX, C), BF16),
        ],
        compiler_params=params(24),
        cost_estimate=QUICK,
        name="middle",
    )(lengths, at, back, latents, spatial_out)
    head, tail, far_up = lax.optimization_barrier((head, tail, far_up))
    count = lax.axis_size("zh") * lax.axis_size("x")
    before = lax.ppermute(tail, SPAN, [(i, i + 1) for i in range(count - 1)])
    behind = lax.ppermute(head, SPAN, [(i + 1, i) for i in range(count - 1)])
    tq, tk, tv = pl.pallas_call(
        time_kernel,
        in_specs=vm(4),
        out_specs=[pl.BlockSpec(memory_space=VMEM)] * 3,
        out_shape=[jax.ShapeDtypeStruct((FR, PX, C), BF16)] * 3,
        compiler_params=params(16),
        cost_estimate=QUICK,
        name="time_qkv",
    )(second, temporal_query, temporal_key, temporal_value)
    half = pair.shape[1] // 2
    ends = (pair_up[:, :half], pair_down[:, half:])
    before, tq, *ends = lax.optimization_barrier((before, tq, *ends))
    far = [shift(ends[0], "x", 1), shift(ends[1], "x", -1)]
    window = FR + 2 * OVL
    late, third = pl.pallas_call(
        temporal_kernel,
        in_specs=[pl.BlockSpec(memory_space=SMEM)] * 3 + vm(9),
        out_specs=[pl.BlockSpec()] * 2,
        out_shape=[jax.ShapeDtypeStruct((FR * PX, C), F32), jax.ShapeDtypeStruct((FR * PX, C), BF16)],
        scratch_shapes=[
            pltpu.VMEM((window, PX, C), BF16),
            pltpu.VMEM((window, PX, C), BF16),
            pltpu.VMEM((FR, PX, C), BF16),
        ],
        compiler_params=params(24),
        cost_estimate=SLOW,
        name="temporal",
    )(lengths, intersection, at, tq, tk, tv, before, behind, middle, temporal_key, temporal_value, temporal_out)
    late_own = after((pair, pair_up, pair_down, far_up), third)
    late_other = [swap(piece, "c") for piece in late_own]
    far = list(after(tuple(far), third))
    far += [swap(piece, "c") for piece in far]
    late = feed(third, late, [part, part_up, part_down, *first, *late_own], ())
    refined = feed(third, late, [*late_other, *far], (lengths, at))
    return refined.reshape(FR, PX, C)


def solution(mesh):
    fine = Mesh(mesh.devices.reshape(4, 4, 4, 2, 2), ("zh", "x", "y", "zl", "c"))
    token = P(SPAN, TOK, None)
    placed = (token,) + (P(),) * 10 + (P(None, SPAN),) * 3
    return jax.shard_map(body, mesh=fine, in_specs=placed, out_specs=token, check_vma=False)
```

```python
import functools

import jax
import jax.numpy as jnp
from jax import lax
from jax.experimental import pallas as pl
from jax.experimental.pallas import tpu as pltpu
from jax.sharding import Mesh
from jax.sharding import PartitionSpec as P

HEADS = 8
OVL = 4
HS = 80
C = 640
FR = 6
HALF = 3
PX = 64
TOKS = 16
PAIR = 16
F32 = jnp.float32
BF16 = jnp.bfloat16
CHUNK = 256
WINDOWS = ((0, (0, 1, 2)), (128, (3,)), (256, (4, 5)), (384, (6, 7)))
SPAN = ("zh", "x")
TOK = ("y", "zl", "c")
SCALE2 = HS ** (-0.5) * 1.4426950408889634
VMEM = pltpu.VMEM
SMEM = pltpu.SMEM
LAYOUT = ((80, 160, 0), (0, 160, 80), (0, 80, 160))


def params(mib=48):
    return pltpu.CompilerParams(vmem_limit_bytes=mib * 1024 * 1024)


def vm(n):
    return [pl.BlockSpec(memory_space=VMEM)] * n


def anys(n):
    return [pl.BlockSpec(memory_space=pl.ANY)] * n


SLOW = pl.CostEstimate(flops=20_000_000_000, bytes_accessed=10_000_000, transcendentals=0)
QUICK = pl.CostEstimate(flops=1000, bytes_accessed=1000, transcendentals=0)


def dot(a, b):
    return jnp.dot(a, b, preferred_element_type=F32)


def dot_t(a, b):
    return lax.dot_general(a, b, (((1,), (1,)), ((), ())), preferred_element_type=F32)


def layer_norm(values):
    center = values - jnp.mean(values, axis=-1, keepdims=True)
    spread = jnp.mean(center * center, axis=-1, keepdims=True)
    return (center * lax.rsqrt(spread + 1e-05)).astype(BF16)


def lanes(shape, start, width):
    lane = lax.broadcasted_iota(jnp.int32, shape, len(shape) - 1)
    return (lane >= start) & (lane < start + width)


def qkv_kernel(x_ref, wq_ref, wk_ref, wv_ref, out_ref, x_s, w_s, o_s, sem, out_sem):
    loads = [pltpu.make_async_copy(x_ref.at[pl.ds(HALF * i, HALF)], x_s.at[i], sem.at[i]) for i in range(2)]
    loads += [pltpu.make_async_copy(w, w_s.at[i], sem.at[2 + i]) for i, w in enumerate((wq_ref, wk_ref, wv_ref))]
    for load in loads:
        load.start()
    stores = []
    pad = jnp.zeros((PX, 256 - 3 * HS), BF16)
    for half in range(2):
        loads[half].wait()
        normed = layer_norm(x_s[half].reshape(HALF * PX, C))
        qkv = []
        for i in range(3):
            if half == 0:
                loads[2 + i].wait()
            qkv.append(dot(normed, w_s[i]).astype(BF16))
        for h in range(HEADS):
            cols = slice(h * HS, (h + 1) * HS)
            for f in range(HALF):
                rows = slice(f * PX, (f + 1) * PX)
                order = sorted(zip(LAYOUT[f], qkv), key=lambda e: e[0])
                parts = [arr[rows, cols] for _, arr in order] + [pad]
                o_s[half * HEADS + h, rows, :] = jnp.concatenate(parts, axis=1)
        at = pl.ds(HEADS * half, HEADS)
        store = pltpu.make_async_copy(o_s.at[at], out_ref.at[at], out_sem.at[half])
        store.start()
        stores.append(store)
    for store in stores:
        store.wait()


def spatial_kernel(x_ref, out_ref, k_ref):
    n = TOKS * PX
    qb = 256
    dst = qb // PX
    for f in range(HALF):
        q_at, k_at, v_at = LAYOUT[f]
        rows = slice(f * PX, (f + 1) * PX)
        x = x_ref[:, rows, :].reshape(n, 256)
        k_ref[f] = pltpu.roll(x.astype(F32), (q_at - k_at) % 256, 1).astype(BF16)
        for i in range(n // qb):
            at = slice(i * dst, (i + 1) * dst)
            xq = x_ref[at, rows, :].reshape(qb, 256)
            xq = jnp.where(lanes((qb, 256), q_at, HS), xq, jnp.zeros_like(xq))
            s = dot_t(xq, k_ref[f])
            top = jnp.max(s, axis=-1, keepdims=True)
            e = jnp.exp2((s - top) * SCALE2)
            r = 1.0 / jnp.sum(e, axis=-1, keepdims=True)
            p = (e * r).astype(BF16)
            ctx = dot(p, x_ref[:, rows, :].reshape(n, 256)).astype(BF16)
            if f > 0:
                ctx = jnp.where(lanes((qb, 256), v_at, HS), ctx, out_ref[at].reshape(qb, 256))
            out_ref[at] = ctx.reshape(dst, PX, 256)


def middle_kernel(len_ref, at_ref, ctx_ref, x_ref, w_ref, mid_ref, second_ref, head_ref, tail_ref):
    rows = []
    for half in range(2):
        for f in range(HALF):
            cols = slice(f * HS, (f + 1) * HS)
            rows.append(jnp.concatenate([ctx_ref[half * HEADS + h, :, cols] for h in range(HEADS)], axis=1))
    context = jnp.concatenate(rows, axis=0)
    middle = x_ref[...].reshape(FR * PX, C) + dot(context, w_ref[...])
    mid_ref[...] = middle
    second = layer_norm(middle).reshape(FR, PX, C)
    second_ref[...] = second
    head_ref[...] = second[:OVL]
    own = len_ref[at_ref[0]]
    for j in range(OVL):
        at = jnp.maximum(own - OVL + j, 0)
        tail_ref[j] = second_ref[at]


def time_kernel(s_ref, wq_ref, wk_ref, wv_ref, q_ref, k_ref, v_ref):
    second = s_ref[...].reshape(FR * PX, C)
    q_ref[...] = dot(second, wq_ref[...]).astype(BF16).reshape(FR, PX, C)
    k_ref[...] = dot(second, wk_ref[...]).astype(BF16).reshape(FR, PX, C)
    v_ref[...] = dot(second, wv_ref[...]).astype(BF16).reshape(FR, PX, C)


def temporal_kernel(
    len_ref, inter_ref, at_ref, q_ref, k_ref, v_ref, prev_ref, next_ref, mid_ref, wk_ref, wv_ref, wo_ref,
    late_ref, third_ref, kw_ref, vw_ref, ctx_ref,
):
    me = at_ref[0]
    spans = len_ref.shape[0]
    own = len_ref[me]
    prev_len = len_ref[jnp.maximum(me - 1, 0)]
    next_len = len_ref[jnp.minimum(me + 1, spans - 1)]
    borrow = inter_ref[me]
    prev = prev_ref[...].reshape(OVL * PX, C)
    after = next_ref[...].reshape(OVL * PX, C)
    kw_ref[:OVL] = dot(prev, wk_ref[...]).astype(BF16).reshape(OVL, PX, C)
    kw_ref[OVL : OVL + FR] = k_ref[...]
    kw_ref[OVL + FR :] = dot(after, wk_ref[...]).astype(BF16).reshape(OVL, PX, C)
    vw_ref[:OVL] = dot(prev, wv_ref[...]).astype(BF16).reshape(OVL, PX, C)
    vw_ref[OVL : OVL + FR] = v_ref[...]
    vw_ref[OVL + FR :] = dot(after, wv_ref[...]).astype(BF16).reshape(OVL, PX, C)

    window = FR + 2 * OVL
    nrow, ncol = FR * PAIR, window * PAIR
    col = lax.broadcasted_iota(jnp.int32, (ncol, nrow), 0)
    row = lax.broadcasted_iota(jnp.int32, (ncol, nrow), 1)
    slot = col // PAIR
    low_prev = jnp.where(me > 0, jnp.maximum(OVL - borrow, OVL - prev_len), OVL)
    high_next = jnp.where(me < spans - 1, jnp.minimum(borrow, next_len), 0)
    live = ((slot >= low_prev) & (slot < OVL + own)) | ((slot >= OVL + FR) & (slot < OVL + FR + high_next))
    bias = jnp.where(live & ((col % PAIR) == (row % PAIR)), 0.0, -1e30)

    for g in range(PX // PAIR):
        at = slice(g * PAIR, (g + 1) * PAIR)
        qg = q_ref[:, at, :].reshape(nrow, C)
        kg = kw_ref[:, at, :].reshape(ncol, C)
        vg = vw_ref[:, at, :].reshape(ncol, C)
        acc = [None] * (C // 128)
        for base, heads in WINDOWS:
            cols = slice(base, base + 256)
            masks = [lanes((nrow, 256), h * HS - base, HS) for h in heads]
            qw = qg[:, cols]
            qs = jnp.concatenate([jnp.where(m, qw, jnp.zeros_like(qw)) for m in masks], axis=0)
            s = dot_t(kg[:, cols], qs) + jnp.concatenate([bias] * len(heads), axis=1)
            top = jnp.max(s, axis=0, keepdims=True)
            e = jnp.exp2((s - top) * SCALE2)
            p = (e * (1.0 / jnp.sum(e, axis=0, keepdims=True))).astype(BF16)
            part = lax.dot_general(p, vg[:, cols], (((0,), (0,)), ((), ())), preferred_element_type=F32)
            merged = None
            for i, m in enumerate(masks):
                one = part[i * nrow : (i + 1) * nrow]
                merged = jnp.where(m, one, 0.0 if merged is None else merged)
            for t in range(2):
                piece = merged[:, t * 128 : (t + 1) * 128]
                i = base // 128 + t
                acc[i] = piece if acc[i] is None else acc[i] + piece
        context = jnp.concatenate(acc, axis=1).astype(BF16)
        ctx_ref[:, at, :] = context.reshape(FR, PAIR, C)
    late = mid_ref[...] + dot(ctx_ref[...].reshape(FR * PX, C), wo_ref[...])
    late_ref[...] = late
    third_ref[...] = layer_norm(late)


def shift(x, axis, by):
    n = lax.axis_size(axis)
    return lax.ppermute(x, axis, [(i, (i + by) % n) for i in range(n)])


def swap(x, axis):
    n = lax.axis_size(axis)
    return lax.ppermute(x, axis, [(i, i ^ 1) for i in range(n)])


def step_z(x):
    n = lax.axis_size("zh")
    pairs = [(2 * k + 1, (2 * k + 2) % (2 * n)) for k in range(n)]
    pairs += [(2 * k, (2 * k - 1) % (2 * n)) for k in range(n)]
    return lax.ppermute(x, ("zh", "zl"), pairs)


def after(x, *others):
    return lax.optimization_barrier((x, *others))[0]


def feed_kernel(count, last, *refs):
    if last:
        len_ref, at_ref, *refs = refs
    third_ref, base_ref, *refs = refs
    pieces = refs[:count]
    out_ref, w_ref, hid_ref, sems = refs[count:]
    loads, ends, end = [], [], 0
    for i, piece in enumerate(pieces):
        n = piece.shape[1]
        load = pltpu.make_async_copy(piece, w_ref.at[:, pl.ds(end, n)], sems.at[i])
        load.start()
        end += n
        loads.append(load)
        ends.append(end)
    third = third_ref[...]
    ready, there = 0, 0
    for start in range(0, end, CHUNK):
        stop = min(start + CHUNK, end)
        while there < stop:
            loads[ready].wait()
            there = ends[ready]
            ready += 1
        at = slice(start, stop)
        gate = dot_t(third, w_ref[1, at])
        gate = 0.5 * gate * (1.0 + lax.erf(gate * (0.5**0.5)))
        hid_ref[:, at] = (dot_t(third, w_ref[0, at]) * gate).astype(BF16)
    total = base_ref[...] + dot(hid_ref[...], w_ref[2])
    if last:
        row = lax.broadcasted_iota(jnp.int32, out_ref.shape, 0)
        total = jnp.where(row < len_ref[at_ref[0]] * PX, total, 0.0)
    out_ref[...] = total


def feed(third, base, pieces, scalars):
    rows = FR * PX
    hidden = sum(p.shape[1] for p in pieces)
    count = len(pieces)
    return pl.pallas_call(
        functools.partial(feed_kernel, count, bool(scalars)),
        in_specs=[pl.BlockSpec(memory_space=SMEM)] * len(scalars) + [pl.BlockSpec()] * 2 + anys(count),
        out_specs=pl.BlockSpec(),
        out_shape=jax.ShapeDtypeStruct((rows, C), F32),
        scratch_shapes=[
            pltpu.VMEM((3, hidden, C), BF16),
            pltpu.VMEM((rows, hidden), BF16),
            pltpu.SemaphoreType.DMA((count,)),
        ],
        compiler_params=params(40),
        cost_estimate=SLOW,
        name="feed_last" if scalars else "feed_first",
    )(*scalars, third, base, *pieces)


def body(
    latents, lengths, intersection, spatial_query, spatial_key, spatial_value, spatial_out,
    temporal_query, temporal_key, temporal_value, temporal_out, feed_value, feed_gate, feed_down,
):
    core = lax.axis_index("c")
    at = (lax.axis_index("zh") * lax.axis_size("x") + lax.axis_index("x")).astype(jnp.int32).reshape(1)
    units = feed_value.shape[1] // 2
    packed = jnp.stack([feed_value.T, feed_gate.T, feed_down.T])
    mine = lax.dynamic_slice_in_dim(packed, core * units, units, axis=1)
    level = lax.axis_index("zl")
    next_1 = step_z(mine)
    part = jnp.concatenate([mine, next_1], axis=1)
    part_up, part_down = shift(part, "x", 1), shift(part, "x", -1)
    far_up = shift(part_up, "x", 1)

    sent = pl.pallas_call(
        qkv_kernel,
        in_specs=anys(4),
        out_specs=pl.BlockSpec(memory_space=pl.ANY),
        out_shape=jax.ShapeDtypeStruct((TOKS, HALF * PX, 256), BF16),
        scratch_shapes=[
            pltpu.VMEM((2, HALF, PX, C), F32),
            pltpu.VMEM((3, C, C), BF16),
            pltpu.VMEM((TOKS, HALF * PX, 256), BF16),
            pltpu.SemaphoreType.DMA((5,)),
            pltpu.SemaphoreType.DMA((2,)),
        ],
        compiler_params=params(60),
        cost_estimate=QUICK,
        name="qkv",
    )(latents, spatial_query, spatial_key, spatial_value)
    got = lax.all_to_all(sent, TOK, 0, 0, tiled=True)
    got, part = lax.optimization_barrier((got, part))
    next_2 = swap(after(next_1, got), "zl")
    half = units // 2
    next_3 = step_z(lax.dynamic_slice_in_dim(next_2, (1 - level) * half, half, axis=1))
    context = pl.pallas_call(
        spatial_kernel,
        in_specs=vm(1),
        out_specs=pl.BlockSpec(),
        out_shape=jax.ShapeDtypeStruct((TOKS, PX, 256), BF16),
        scratch_shapes=[pltpu.VMEM((HALF, TOKS * PX, 256), BF16)],
        compiler_params=params(28),
        cost_estimate=QUICK,
        name="spatial",
    )(got)
    back = lax.all_to_all(context, TOK, 0, 0, tiled=True)
    next_4 = swap(next_3, "zl")
    pair = jnp.concatenate([next_2, next_3, next_4], axis=1)
    pair_up, pair_down = shift(pair, "x", 1), shift(pair, "x", -1)
    first = [swap(piece, "c") for piece in (part, part_up, part_down)]
    back, *first = lax.optimization_barrier((back, *first))
    middle, second, head, tail = pl.pallas_call(
        middle_kernel,
        in_specs=[pl.BlockSpec(memory_space=SMEM)] * 2 + vm(3),
        out_specs=[pl.BlockSpec()] + [pl.BlockSpec(memory_space=VMEM)] * 3,
        out_shape=[
            jax.ShapeDtypeStruct((FR * PX, C), F32),
            jax.ShapeDtypeStruct((FR, PX, C), BF16),
            jax.ShapeDtypeStruct((OVL, PX, C), BF16),
            jax.ShapeDtypeStruct((OVL, PX, C), BF16),
        ],
        compiler_params=params(24),
        cost_estimate=QUICK,
        name="middle",
    )(lengths, at, back, latents, spatial_out)
    head, tail, far_up = lax.optimization_barrier((head, tail, far_up))
    count = lax.axis_size("zh") * lax.axis_size("x")
    before = lax.ppermute(tail, SPAN, [(i, i + 1) for i in range(count - 1)])
    behind = lax.ppermute(head, SPAN, [(i + 1, i) for i in range(count - 1)])
    tq, tk, tv = pl.pallas_call(
        time_kernel,
        in_specs=vm(4),
        out_specs=[pl.BlockSpec(memory_space=VMEM)] * 3,
        out_shape=[jax.ShapeDtypeStruct((FR, PX, C), BF16)] * 3,
        compiler_params=params(16),
        cost_estimate=QUICK,
        name="time_qkv",
    )(second, temporal_query, temporal_key, temporal_value)
    half = pair.shape[1] // 2
    ends = (pair_up[:, :half], pair_down[:, half:])
    tq, *ends = lax.optimization_barrier((tq, *ends))
    far = [shift(ends[0], "x", 1), shift(ends[1], "x", -1)]
    window = FR + 2 * OVL
    late, third = pl.pallas_call(
        temporal_kernel,
        in_specs=[pl.BlockSpec(memory_space=SMEM)] * 3 + vm(9),
        out_specs=[pl.BlockSpec()] * 2,
        out_shape=[jax.ShapeDtypeStruct((FR * PX, C), F32), jax.ShapeDtypeStruct((FR * PX, C), BF16)],
        scratch_shapes=[
            pltpu.VMEM((window, PX, C), BF16),
            pltpu.VMEM((window, PX, C), BF16),
            pltpu.VMEM((FR, PX, C), BF16),
        ],
        compiler_params=params(24),
        cost_estimate=SLOW,
        name="temporal",
    )(lengths, intersection, at, tq, tk, tv, before, behind, middle, temporal_key, temporal_value, temporal_out)
    late_own = after((pair, pair_up, pair_down, far_up), third)
    late_other = [swap(piece, "c") for piece in late_own]
    far = list(after(tuple(far), third))
    far += [swap(piece, "c") for piece in far]
    late = feed(third, late, [part, part_up, part_down, *first, *late_own], ())
    refined = feed(third, late, [*late_other, *far], (lengths, at))
    return refined.reshape(FR, PX, C)


def solution(mesh):
    fine = Mesh(mesh.devices.reshape(4, 4, 4, 2, 2), ("zh", "x", "y", "zl", "c"))
    token = P(SPAN, TOK, None)
    placed = (token,) + (P(),) * 10 + (P(None, SPAN),) * 3
    return jax.shard_map(body, mesh=fine, in_specs=placed, out_specs=token, check_vma=False)
```
